512 devices in a mesh: dp: 16 (over z, x_hi), wide: 32 (over y, x_lo, core).
Axes of the slice: x: 4 (x_hi: 2, x_lo: 2; x = x_hi * 2 + x_lo), y: 8, z: 8, core: 2. Of those that a mesh axis runs over, the one named last changes fastest.
Arguments:
- activations: bfloat16 [65536, 16384], P(('dp', 'wide')), may hold values from -24 to 24
- output_gradients: bfloat16 [65536, 256], P(('dp', 'wide')), may hold values from -0.0234375 to 0.0234375
- frozen_span_rows: bfloat16 [4, 2, 64, 16384], P(None, None, 'wide'), may hold values from -0.046875 to 0.046875
- span_owner_slab: int32 [4], replicated, may hold values from 0 to 3, each once
- adapter_down_factor: bfloat16 [16384, 64], P('wide'), may hold values from -0.046875 to 0.046875
- adapter_up_factor: bfloat16 [64, 256], replicated, may hold values from -0.75 to 0.75
- completion_token_counts: int32 [1024], P(('dp', 'wide')), may hold values from 1 to 64
- balance_slot_plan: int32 [16, 4096], P('dp'), may hold values from 0 to 4095, as said below
Outputs:
- adapter_down_gradient: float32 [16384, 64], P('wide')
- adapter_up_gradient: float32 [64, 256], replicated
The draws below stay inside these ranges and needn't reach their ends.
Inputs may be any that keep to these rules, and one draw needn't show every extreme that they name: `balance_slot_plan`: for each replica, a permutation of the 4096 slots; slot s lies on device s // 128 of wide, and every device of wide sends exactly 4 of its rows to every device of wide.
All inputs are finite; a program needn't handle non-finite values.
Results may differ from the reference program's by a relative error of at most 0.0095.
Values may be sent and summed in bfloat16 or wider, within the bound.
No kernel may reach another device: no remote copies, remote signals or barrier semaphores. Data moves between devices by JAX's collectives and lax.ppermute only.
A program may use at most 128 MiB of HBM per device.

```python
import jax
import jax.numpy as jnp
from jax import lax

MODEL_WIDTH = 16384
ADAPTER_RANK = 64
UNITS = 64
SPANS = 4
CPR = 2
DEVICE_ROWS = 128
SEG = 64
HIDDEN_TOTAL = 256
TOKENS = 65536
N_DP = 16
N_WIDE = 32


def draw_balance_slot_plan(key, part):
    key = jax.random.fold_in(key, 11)
    piece_rows = DEVICE_ROWS // N_WIDE
    keys = jax.random.split(key, N_DP * N_WIDE * 2)
    perms = jax.vmap(lambda one_key: jax.random.permutation(one_key, DEVICE_ROWS))(keys).reshape(N_DP, 2, N_WIDE, DEVICE_ROWS).astype(jnp.int32)
    sends = perms[:, 0]
    layouts = perms[:, 1]
    offsets = jnp.arange(DEVICE_ROWS, dtype=jnp.int32)
    dest_dev = offsets // piece_rows
    within = jnp.arange(N_WIDE, dtype=jnp.int32)[:, None] * piece_rows + (offsets % piece_rows)[None, :]
    groups = jnp.arange(N_DP, dtype=jnp.int32)[:, None, None]
    slots = dest_dev[None, None, :] * DEVICE_ROWS + layouts[groups, dest_dev[None, None, :], within[None, :, :]]
    sources = jnp.arange(N_WIDE, dtype=jnp.int32)[None, :, None] * DEVICE_ROWS + sends
    plan = jnp.zeros((N_DP, N_WIDE * DEVICE_ROWS), jnp.int32)
    return plan.at[groups, sources].set(slots)


def touch_ends(drawn, key, smallest, largest):
    dims = drawn.shape
    place = [jax.random.randint(jax.random.fold_in(key, axis), (), 0, dims[axis]) for axis in range(len(dims))]
    drawn = drawn.at[tuple(place)].set(smallest)
    longest = dims.index(max(dims))
    place[longest] = (place[longest] + 1) % dims[longest]
    return drawn.at[tuple(place)].set(largest)


def strengthened(values, stream_key, source, target, parts, factor):
    owner, partner = [(jnp.arange(values.shape[dim]) // (values.shape[dim] // parts)).reshape([-1 if axis == dim else 1 for axis in range(values.ndim)]) for dim in (source, target)]
    chosen = jax.random.permutation(stream_key, parts)[partner]
    strong = (owner == chosen) | (owner == (partner + parts // 2) % parts)
    return jnp.where(strong, factor * values, values)


def steps_of(own_key, shape, shards, least, top_value):
    loudness, own = 1.0, jax.random.fold_in(own_key, 6)
    for axis_at, blocks in shards:
        draws = jnp.exp(jax.random.uniform(jax.random.fold_in(own, axis_at), (blocks,), jnp.float32, least / len(shards), top_value / len(shards)))
        loudness = loudness * jnp.repeat(draws, shape[axis_at] // blocks).reshape([-1 if axis == axis_at else 1 for axis in range(len(shape))])
    return loudness


def scatter_about(stream_key, dims, scale, reach, pieces=(), kind=jnp.bfloat16):
    drawn = jax.random.normal(stream_key, dims, jnp.float32) * scale
    if len(pieces) > 0:
        drawn = steps_of(stream_key, dims, pieces, -0.22, 0.18) * drawn
    return jnp.clip(drawn, min=-reach, max=reach).astype(kind)


def gaussian_with(stream_key, dims, width, reach, shards, heavy, kind=jnp.bfloat16):
    drawn = width * jax.random.normal(stream_key, dims, jnp.float32)
    if shards:
        drawn = drawn * steps_of(stream_key, dims, shards, -0.22, 0.18)
    return jnp.clip(strengthened(drawn, jax.random.fold_in(stream_key, 3), *heavy), -reach, reach).astype(kind)


def setup_inputs(seed: int = 0) -> dict:
    seeds = jax.random.split(jax.random.key(seed), 9)
    activations = gaussian_with(seeds[0], (TOKENS, MODEL_WIDTH), 1.0, 24.0, ((0, 512),), (0, 1, 512, 6.0))
    output_gradients = scatter_about(seeds[1], (TOKENS, HIDDEN_TOTAL), (TOKENS ** -0.5), 0.0234375, ((0, 512),))
    frozen_span_rows = scatter_about(seeds[2], (SPANS, 2, UNITS, MODEL_WIDTH), MODEL_WIDTH ** -0.5, 0.046875, ((2, 32),))
    span_owner_slab = jax.random.permutation(seeds[3], SPANS).astype(jnp.int32)
    adapter_down_factor = scatter_about(seeds[4], (MODEL_WIDTH, ADAPTER_RANK), MODEL_WIDTH ** -0.5, 0.046875, ((0, 32),))
    adapter_up_factor = scatter_about(seeds[5], (ADAPTER_RANK, HIDDEN_TOTAL), ADAPTER_RANK ** -0.5, 0.75)
    completion_token_counts = touch_ends(jax.random.randint(seeds[6], (N_DP * N_WIDE * CPR,), 1, SEG + 1), jax.random.fold_in(seeds[6], 1), 1, SEG).astype(jnp.int32)
    balance_slot_plan = draw_balance_slot_plan(jax.random.fold_in(seeds[8], 71), 0)
    return {"activations": activations, "output_gradients": output_gradients, "frozen_span_rows": frozen_span_rows, "span_owner_slab": span_owner_slab, "adapter_down_factor": adapter_down_factor, "adapter_up_factor": adapter_up_factor, "completion_token_counts": completion_token_counts, "balance_slot_plan": balance_slot_plan}


def reference(activations, output_gradients, frozen_span_rows, span_owner_slab, adapter_down_factor, adapter_up_factor, completion_token_counts, balance_slot_plan):
    seg_rows = DEVICE_ROWS // CPR
    row_count = activations.shape[0]
    position = jnp.arange(row_count, dtype=jnp.int32)
    live_rows = (position % seg_rows) < jnp.repeat(completion_token_counts, seg_rows, total_repeat_length=row_count)
    masked_rows = jnp.where(live_rows[:, None], activations, jnp.zeros_like(activations))
    group_rows = N_WIDE * DEVICE_ROWS
    target_slot = ((position // group_rows) * group_rows + balance_slot_plan.reshape(-1)).astype(jnp.int32)
    balanced_rows = jnp.zeros_like(masked_rows).at[target_slot].set(masked_rows)
    ordered_rows = frozen_span_rows[span_owner_slab]
    gate_matrix = ordered_rows[:, 0].reshape(HIDDEN_TOTAL, MODEL_WIDTH)
    up_matrix = ordered_rows[:, 1].reshape(HIDDEN_TOTAL, MODEL_WIDTH)
    adapter_product = jnp.dot(balanced_rows, adapter_down_factor, preferred_element_type=jnp.float32).astype(jnp.bfloat16)
    gate_preactivation = jnp.dot(balanced_rows, gate_matrix.T, preferred_element_type=jnp.float32) + jnp.dot(adapter_product, adapter_up_factor, preferred_element_type=jnp.float32)
    up_preactivation = jnp.dot(balanced_rows, up_matrix.T, preferred_element_type=jnp.float32)
    sigmoid_gate = jax.nn.sigmoid(gate_preactivation)
    gate_gradient = (output_gradients.astype(jnp.float32) * up_preactivation * sigmoid_gate * (1.0 + gate_preactivation * (1.0 - sigmoid_gate))).astype(jnp.bfloat16)
    adapter_up_gradient = jnp.dot(adapter_product.T, gate_gradient, preferred_element_type=jnp.float32)
    adapter_product_gradient = jnp.dot(gate_gradient, adapter_up_factor.T, preferred_element_type=jnp.float32).astype(jnp.bfloat16)

    def device_accumulate(carry, device_index):
        input_rows = lax.dynamic_slice_in_dim(balanced_rows, device_index * DEVICE_ROWS, DEVICE_ROWS, 0)
        rows_z = lax.dynamic_slice_in_dim(adapter_product_gradient, device_index * DEVICE_ROWS, DEVICE_ROWS, 0)
        partial_term = jnp.dot(input_rows.T, rows_z, preferred_element_type=jnp.float32)
        partial_term = lax.optimization_barrier(partial_term.astype(jnp.bfloat16)).astype(jnp.float32)
        return carry + partial_term, None

    adapter_down_gradient, unused_value = lax.scan(device_accumulate, jnp.zeros((MODEL_WIDTH, ADAPTER_RANK), jnp.float32), jnp.arange(N_DP * N_WIDE, dtype=jnp.int32))
    return adapter_down_gradient, adapter_up_gradient
```

```python
import functools

import jax
import jax.numpy as jnp
from jax import lax
from jax.experimental import pallas as pl
from jax.experimental.pallas import tpu as pltpu
from jax.sharding import Mesh
from jax.sharding import PartitionSpec as P

F32 = jnp.float32
BF16 = jnp.bfloat16
DP = ("z", "xh")
WIDE = ("y", "xl", "core")
RING = ("xh", "xl")
REPLICAS = ("z", "xh", "y")
EVERY = ("z", "xh", "y", "xl", "core")
VMEM_LIMIT = 40 * 1024 * 1024
NT = (((1,), (1,)), ((), ()))
TN = (((0,), (0,)), ((), ()))


def shift(array, axes, step):
    size = lax.axis_size(axes)
    return lax.ppermute(array, axes, [(i, (i + step) % size) for i in range(size)])


def exchange(array, axes):
    return lax.all_to_all(array, axes, split_axis=0, concat_axis=0, tiled=True)


def params():
    return pltpu.CompilerParams(vmem_limit_bytes=VMEM_LIMIT)


def split_rows_kernel(core_ref, x_ref, own_a, own_b, other_a, other_b, *, block):
    core = core_ref[0]
    half = x_ref.shape[0] // 2
    for xl in range(2):
        mine = pl.multiple_of(xl * 2 * block + core * block, block)
        his = pl.multiple_of(xl * 2 * block + (1 - core) * block, block)
        own_a[xl, 0] = x_ref[:half, pl.ds(mine, block)]
        own_b[xl, 0] = x_ref[half:, pl.ds(mine, block)]
        other_a[xl, 0] = x_ref[:half, pl.ds(his, block)]
        other_b[xl, 0] = x_ref[half:, pl.ds(his, block)]


def split_rows(x, core, ys, block):
    rows, width = x.shape
    half = rows // 2
    shape = jax.ShapeDtypeStruct((2, ys // 4, half, 4 * block), BF16)
    spec = pl.BlockSpec((2, 1, half, block), lambda y, c: (0, y // 4, 0, y % 4))
    parts = pl.pallas_call(
        functools.partial(split_rows_kernel, block=block),
        grid_spec=pltpu.PrefetchScalarGridSpec(
            num_scalar_prefetch=1,
            grid=(ys,),
            in_specs=[pl.BlockSpec((rows, 4 * block), lambda y, c: (0, y))],
            out_specs=[spec] * 4,
        ),
        out_shape=[shape] * 4,
        compiler_params=params(),
        cost_estimate=pl.CostEstimate(flops=0, bytes_accessed=rows * width * 4, transcendentals=0),
        name="split_rows",
    )(core, x)
    return [part.reshape(2 * (ys // 4), half, 4 * block) for part in parts]


def split_weights_kernel(w_ref, out_ref, *, block):
    spans, _, units, _ = w_ref.shape
    rows = jnp.concatenate(
        [w_ref[s, j].astype(F32) for j in range(2) for s in range(spans)], axis=0
    ).astype(BF16)
    for parity in range(2):
        for xl in range(2):
            at = (xl * 2 + parity) * block
            out_ref[parity, xl, 0] = rows[:, at : at + block]


def split_weights(w, ys, block):
    spans, _, units, width = w.shape
    n = 2 * spans * units
    out = pl.pallas_call(
        functools.partial(split_weights_kernel, block=block),
        grid=(ys,),
        in_specs=[pl.BlockSpec((spans, 2, units, 4 * block), lambda y: (0, 0, 0, y))],
        out_specs=pl.BlockSpec((2, 2, 1, n, block), lambda y: (0, 0, y // 4, 0, y % 4)),
        out_shape=jax.ShapeDtypeStruct((2, 2, ys // 4, n, 4 * block), BF16),
        compiler_params=params(),
        cost_estimate=pl.CostEstimate(flops=0, bytes_accessed=w.size * 4, transcendentals=0),
        name="split_weights",
    )(w)
    return out.reshape(2, 2 * (ys // 4), n, 4 * block)


def products_kernel(*refs, block):
    x_refs, (w_ref, down_ref, out_ref) = refs[:8], refs[8:]
    x = jnp.concatenate([r[0] for r in x_refs], axis=0)
    w = w_ref[...].reshape(-1, w_ref.shape[-1])
    down = jnp.concatenate(
        [
            jnp.concatenate(
                [down_ref[y, :, t * block : (t + 1) * block] for t in range(4)], axis=0
            )
            for y in range(4)
        ],
        axis=1,
    )
    units = w.shape[0]
    wide = lax.dot_general(x, w, NT, preferred_element_type=F32)
    low = lax.dot_general(x, down, NT, preferred_element_type=F32)

    @pl.when(pl.program_id(0) == 0)
    def _():
        out_ref[:, :units] = wide
        out_ref[:, units:] = low

    @pl.when(pl.program_id(0) > 0)
    def _():
        out_ref[:, :units] += wide
        out_ref[:, units:] += low


def products(xs, gathered, n, rank, block):
    chunks, part, lanes = xs[0].shape
    ys = gathered.shape[0]
    units = ys * 2 * n
    x_spec = pl.BlockSpec((1, part, lanes), lambda k: (k, 0, 0))
    per = chunks // 2
    return pl.pallas_call(
        functools.partial(products_kernel, block=block),
        grid=(chunks,),
        in_specs=[x_spec] * 8
        + [
            pl.BlockSpec((ys, 2 * n, lanes), lambda k: (0, k, 0)),
            pl.BlockSpec((4, rank // 4, lanes), lambda k: (k % per, 2 * chunks + k // per, 0)),
        ],
        out_specs=pl.BlockSpec((8 * part, units + rank), lambda k: (0, 0)),
        out_shape=jax.ShapeDtypeStruct((8 * part, units + rank), F32),
        compiler_params=params(),
        cost_estimate=pl.CostEstimate(
            flops=2 * 8 * part * chunks * lanes * (units + rank),
            bytes_accessed=(8 * part + units + rank) * chunks * lanes * 2,
            transcendentals=0,
        ),
        name="products",
    )(*xs, gathered, gathered)


def swap_pairs(ref, part):
    return jnp.concatenate(
        [ref[(i ^ 1) * part : ((i ^ 1) + 1) * part] for i in range(8)], axis=0
    )


def gate_kernel(mine_ref, his_ref, cot_ref, pick_ref, up_ref, low_ref, up_grad_ref, *, n, part):
    units = pick_ref.shape[1]
    total = mine_ref[...] + swap_pairs(his_ref, part)
    low = total[:, units:].astype(BF16)
    pick = pick_ref[...]
    up = jnp.dot(up_ref[...], pick, preferred_element_type=F32).astype(BF16)
    cot = jnp.dot(cot_ref[...], pick, preferred_element_type=F32)
    both = total[:, :units]
    gate = both + jnp.dot(low, up, preferred_element_type=F32)
    upper = pltpu.roll(both, units - n // 2, 1)
    s = jax.nn.sigmoid(gate)
    grad = (cot * upper * s * (1.0 + gate * (1.0 - s))).astype(BF16)
    low_ref[...] = lax.dot_general(grad, up, NT, preferred_element_type=F32)
    ordered = lax.dot_general(grad, pick, NT, preferred_element_type=F32).astype(BF16)
    first = [i for i in range(8) if i % 2 == 0]
    low_m = jnp.concatenate([low[i * part : (i + 1) * part] for i in first], axis=0)
    ordered_m = jnp.concatenate([ordered[i * part : (i + 1) * part] for i in first], axis=0)
    up_grad_ref[...] = lax.dot_general(low_m, ordered_m, TN, preferred_element_type=F32)


def gate_stage(mine, his, cot, pick, up, n):
    rows = mine.shape[0]
    rank, hidden = up.shape
    vm = pl.BlockSpec(memory_space=pltpu.VMEM)
    return pl.pallas_call(
        functools.partial(gate_kernel, n=n, part=rows // 8),
        in_specs=[vm] * 5,
        out_specs=[vm, vm],
        out_shape=[
            jax.ShapeDtypeStruct((rows, rank), F32),
            jax.ShapeDtypeStruct((rank, hidden), F32),
        ],
        compiler_params=params(),
        cost_estimate=pl.CostEstimate(
            flops=2 * rows * hidden * (2 * hidden + 3 * rank),
            bytes_accessed=rows * hidden * 12,
            transcendentals=rows * hidden,
        ),
        name="gate_stage",
    )(mine, his, cot, pick, up)


def down_kernel(xl_ref, *refs):
    x_refs, (mine_ref, plus_ref, minus_ref, out_ref) = refs[:8], refs[8:]
    half = plus_ref.shape[0]
    low = jnp.concatenate(
        [mine_ref[:half] + plus_ref[...], mine_ref[half:] + minus_ref[...]], axis=0
    ).astype(BF16)
    x = jnp.concatenate([r[0] for r in x_refs], axis=0)
    out_ref[0] = lax.dot_general(low, x, TN, preferred_element_type=F32).astype(BF16)


def down_terms(xs, xl, mine, plus, minus, ys, block):
    chunks, part, lanes = xs[0].shape
    per = chunks // 2
    rows, rank = mine.shape
    x_spec = pl.BlockSpec((1, part, block), lambda y, v: (v[0] * per + y // 4, 0, y % 4))
    full = pl.BlockSpec((rows, rank), lambda y, v: (0, 0))
    half = pl.BlockSpec((rows // 2, rank), lambda y, v: (0, 0))
    return pl.pallas_call(
        down_kernel,
        grid_spec=pltpu.PrefetchScalarGridSpec(
            num_scalar_prefetch=1,
            grid=(ys,),
            in_specs=[x_spec] * 8 + [full, half, half],
            out_specs=pl.BlockSpec((1, rank, block), lambda y, v: (y, 0, 0)),
        ),
        out_shape=jax.ShapeDtypeStruct((ys, rank, block), BF16),
        compiler_params=params(),
        cost_estimate=pl.CostEstimate(
            flops=2 * rows * rank * ys * block,
            bytes_accessed=(rows + rank) * ys * block * 2,
            transcendentals=0,
        ),
        name="down_terms",
    )(xl, *xs, mine, plus, minus)


def chosen(condition):
    return condition.astype(BF16)


def cotangent_rows(grads, plan, counts, place):
    rows = grads.shape[0]
    lanes = lax.axis_size(WIDE)
    seg = rows // counts.shape[0]
    local = jnp.arange(rows, dtype=jnp.int32)
    slots = lax.dynamic_slice_in_dim(plan, place * rows, rows, 0)
    rank = jnp.sum((slots[None, :] < slots[:, None]).astype(jnp.int32), axis=1)
    owner = jnp.arange(plan.shape[0], dtype=jnp.int32) // rows
    held = plan[None, :] == (place * rows + local)[:, None]
    source = jnp.sum(jnp.where(held, owner[None, :], 0), axis=1)
    before = (source[None, :] == source[:, None]) & (local[None, :] < local[:, None])
    spot = source * (rows // lanes) + jnp.sum(before.astype(jnp.int32), axis=1)
    sent = jnp.dot(
        chosen(spot[None, :] == local[:, None]), grads, preferred_element_type=F32
    ).astype(BF16)
    back = exchange(sent, WIDE)
    live = local % seg < jnp.repeat(counts, seg, total_repeat_length=rows)
    pick = (rank[:, None] == local[None, :]) & live[:, None]
    return jnp.dot(chosen(pick), back, preferred_element_type=F32).astype(BF16)


def unit_order(slab, xl, ys, n, hidden):
    spans = slab.shape[0]
    per_span = hidden // spans
    units = n // (2 * spans)
    at = jnp.arange(ys * 2 * n, dtype=jnp.int32)
    y, core = at // (2 * n), at // n % 2
    gate, span, unit = at // (n // 2) % 2 == 0, at // units % spans, at % units
    k = ((y * 2 + xl) * 2 + core) * units + unit
    h = jnp.arange(hidden, dtype=jnp.int32)
    stored = jnp.repeat(slab, per_span, total_repeat_length=hidden)
    return chosen(
        gate[None, :]
        & (stored[:, None] == span[None, :])
        & ((h % per_span)[:, None] == k[None, :])
    )


def shards(x, grads, frozen, slab, down, up, counts, plan):
    ys = lax.axis_size("y")
    lanes = lax.axis_size(WIDE)
    copies = lax.axis_size(DP)
    xl, core = lax.axis_index("xl"), lax.axis_index("core")
    rows, width = x.shape
    block, rank = down.shape
    hidden = up.shape[1]
    half = rows // 2
    n = 2 * frozen.shape[0] * frozen.shape[2]
    core_id = core.astype(jnp.int32).reshape(1)
    xl_id = xl.astype(jnp.int32).reshape(1)

    swapped = exchange(split_weights(frozen, ys, block), "core")
    chunks = swapped.shape[1]
    down_rows = down.T.reshape(4, rank // 4, block).transpose(1, 0, 2).reshape(rank // 4, 4 * block)
    near_down = shift(down_rows, "xl", 1)
    both_down = jnp.where(
        xl == 0,
        jnp.concatenate([down_rows, near_down], axis=0),
        jnp.concatenate([near_down, down_rows], axis=0),
    )
    sent = jnp.concatenate(
        [swapped.transpose(1, 0, 2, 3).reshape(chunks * 2 * n, 4 * block), both_down], axis=0
    )
    gathered = lax.all_gather(sent[None], "y", axis=0, tiled=True)

    own_a, own_b, other_a, other_b = split_rows(x, core_id, ys, block)
    next_own = shift(own_a, RING, 1)
    prev_own = shift(own_b, RING, -1)
    pair_a = shift(other_a, "core", 1)
    pair_b = shift(other_b, "core", 1)
    next_pair = shift(pair_a, RING, 1)
    prev_pair = shift(pair_b, RING, -1)
    xs = [own_a, pair_a, prev_own, prev_pair, next_own, next_pair, own_b, pair_b]

    cot = cotangent_rows(grads, plan[0], counts, lax.axis_index(WIDE))
    cot_pair = shift(cot, "core", 1)
    cot_a = jnp.concatenate([cot[:half], cot_pair[:half]], axis=0)
    cot_b = jnp.concatenate([cot[half:], cot_pair[half:]], axis=0)
    cots = jnp.concatenate([cot_a, shift(cot_b, RING, -1), shift(cot_a, RING, 1), cot_b], axis=0)

    mine = products(xs, gathered, n, rank, block)
    his = shift(mine, "core", 1)
    low, up_part = gate_stage(mine, his, cots, unit_order(slab, xl, ys, n, hidden), up, n)

    group = low.shape[0] // 2
    plus = shift(low[group:], RING, -1)
    minus = shift(low[:group], RING, 1)

    up_share = exchange(up_part, WIDE).reshape(lanes, rank // lanes, hidden).sum(0)
    up_all = exchange(jnp.tile(up_share, (copies, 1)), DP)
    up_share = up_all.reshape(copies, rank // lanes, hidden).sum(0)
    up_grad = exchange(jnp.tile(up_share, (lanes, 1)), WIDE)

    terms = down_terms(xs, xl_id, low, plus, minus, ys, block)
    terms = terms.reshape(ys, copies, rank // copies, block).transpose(1, 0, 2, 3)
    terms = exchange(terms.reshape(copies * ys, rank // copies, block), REPLICAS)
    share = terms.astype(F32).sum(0)
    full = exchange(jnp.tile(share[None], (copies, 1, 1)), DP)
    return full.reshape(rank, block).T, up_grad


def solution(mesh):
    dp, wide = mesh.devices.shape
    fine = Mesh(mesh.devices.reshape(dp // 2, 2, wide // 4, 2, 2), EVERY)
    placed = (
        P(EVERY, None),
        P(EVERY, None),
        P(None, None, WIDE, None),
        P(),
        P(WIDE, None),
        P(),
        P(EVERY),
        P(DP, None),
    )
    return jax.shard_map(
        shards, mesh=fine, in_specs=placed, out_specs=(P(WIDE, None), P()), check_vma=False
    )
```

```python
import functools

import jax
import jax.numpy as jnp
from jax import lax
from jax.experimental import pallas as pl
from jax.experimental.pallas import tpu as pltpu
from jax.sharding import Mesh
from jax.sharding import PartitionSpec as P

F32 = jnp.float32
BF16 = jnp.bfloat16
DP = ("z", "xh")
WIDE = ("y", "xl", "core")
RING = ("xh", "xl")
REPLICAS = ("z", "xh", "y")
EVERY = ("z", "xh", "y", "xl", "core")
MIB = 1024 * 1024
NT = (((1,), (1,)), ((), ()))
TN = (((0,), (0,)), ((), ()))


def shift(array, axes, step):
    size = lax.axis_size(axes)
    return lax.ppermute(array, axes, [(i, (i + step) % size) for i in range(size)])


def exchange(array, axes):
    return lax.all_to_all(array, axes, split_axis=0, concat_axis=0, tiled=True)


def params(mib):
    return pltpu.CompilerParams(vmem_limit_bytes=mib * MIB)


def split_rows_kernel(core_ref, x_ref, own_a, own_b, other_a, other_b, *, block):
    core = core_ref[0]
    half = x_ref.shape[0] // 2
    for xl in range(2):
        mine = pl.multiple_of(xl * 2 * block + core * block, block)
        his = pl.multiple_of(xl * 2 * block + (1 - core) * block, block)
        own_a[xl, 0] = x_ref[:half, pl.ds(mine, block)]
        own_b[xl, 0] = x_ref[half:, pl.ds(mine, block)]
        other_a[xl, 0] = x_ref[:half, pl.ds(his, block)]
        other_b[xl, 0] = x_ref[half:, pl.ds(his, block)]


def split_rows(x, core, ys, block):
    rows, width = x.shape
    half = rows // 2
    shape = jax.ShapeDtypeStruct((2, ys // 4, half, 4 * block), BF16)
    spec = pl.BlockSpec((2, 1, half, block), lambda y, c: (0, y // 4, 0, y % 4))
    parts = pl.pallas_call(
        functools.partial(split_rows_kernel, block=block),
        grid_spec=pltpu.PrefetchScalarGridSpec(
            num_scalar_prefetch=1,
            grid=(ys,),
            in_specs=[pl.BlockSpec((rows, 4 * block), lambda y, c: (0, y))],
            out_specs=[spec] * 4,
        ),
        out_shape=[shape] * 4,
        compiler_params=params(24),
        cost_estimate=pl.CostEstimate(flops=0, bytes_accessed=rows * width * 4, transcendentals=0),
        name="split_rows",
    )(core, x)
    return [part.reshape(2 * (ys // 4), half, 4 * block) for part in parts]


def split_weights_kernel(w_ref, out_ref, *, block):
    spans, _, units, _ = w_ref.shape
    rows = jnp.concatenate(
        [w_ref[s, j].astype(F32) for j in range(2) for s in range(spans)], axis=0
    ).astype(BF16)
    for parity in range(2):
        for xl in range(2):
            for y in range(4):
                at = ((y * 2 + xl) * 2 + parity) * block
                out_ref[parity, xl, 0, :, y * block : (y + 1) * block] = rows[:, at : at + block]


def split_weights(w, ys, block):
    spans, _, units, width = w.shape
    n = 2 * spans * units
    out = pl.pallas_call(
        functools.partial(split_weights_kernel, block=block),
        grid=(ys // 4,),
        in_specs=[pl.BlockSpec((spans, 2, units, 16 * block), lambda y: (0, 0, 0, y))],
        out_specs=pl.BlockSpec((2, 2, 1, n, 4 * block), lambda y: (0, 0, y, 0, 0)),
        out_shape=jax.ShapeDtypeStruct((2, 2, ys // 4, n, 4 * block), BF16),
        compiler_params=params(24),
        cost_estimate=pl.CostEstimate(flops=0, bytes_accessed=w.size * 4, transcendentals=0),
        name="split_weights",
    )(w)
    return out.reshape(2, 2 * (ys // 4), n, 4 * block)


def products_kernel(*refs, block, rank):
    x_refs, (w_ref, down_ref, out_ref) = refs[:8], refs[8:]
    x = jnp.concatenate([r[0] for r in x_refs], axis=0)
    w = w_ref[...].reshape(-1, w_ref.shape[-1])
    down = jnp.concatenate(
        [
            jnp.concatenate(
                [down_ref[y, :, t * block : (t + 1) * block] for t in range(4)], axis=0
            )
            for y in range(4)
        ],
        axis=1,
    )
    units = w.shape[0]
    wide = lax.dot_general(x, w, NT, preferred_element_type=F32)
    low = lax.dot_general(x, down, NT, preferred_element_type=F32)

    @pl.when(pl.program_id(0) == 0)
    def _():
        out_ref[:, :units] = wide
        out_ref[:, units : units + rank] = low
        out_ref[:, units + rank :] = jnp.zeros_like(out_ref[:, units + rank :])

    @pl.when(pl.program_id(0) > 0)
    def _():
        out_ref[:, :units] += wide
        out_ref[:, units : units + rank] += low


def products(xs, gathered, n, rank, block):
    chunks, part, lanes = xs[0].shape
    ys = gathered.shape[0]
    units = ys * 2 * n
    columns = units + pl.cdiv(rank, 128) * 128
    x_spec = pl.BlockSpec((1, part, lanes), lambda k: (k, 0, 0))
    per = chunks // 2
    return pl.pallas_call(
        functools.partial(products_kernel, block=block, rank=rank),
        grid=(chunks,),
        in_specs=[x_spec] * 8
        + [
            pl.BlockSpec((ys, 2 * n, lanes), lambda k: (0, k, 0)),
            pl.BlockSpec((4, rank // 4, lanes), lambda k: (k % per, 2 * chunks + k // per, 0)),
        ],
        out_specs=pl.BlockSpec((8 * part, columns), lambda k: (0, 0)),
        out_shape=jax.ShapeDtypeStruct((8 * part, columns), F32),
        compiler_params=params(60),
        cost_estimate=pl.CostEstimate(
            flops=2 * 8 * part * chunks * lanes * (units + rank),
            bytes_accessed=(8 * part + units + rank) * chunks * lanes * 2,
            transcendentals=0,
        ),
        name="products",
    )(*xs, gathered, gathered)


def swap_pairs(ref, part):
    return jnp.concatenate(
        [ref[(i ^ 1) * part : ((i ^ 1) + 1) * part] for i in range(8)], axis=0
    )


def gate_kernel(mine_ref, his_ref, a_ref, next_b_ref, prev_a_ref, b_ref, pick_ref, up_ref,
                plus_ref, minus_ref, *, n, part, rank):
    units = pick_ref.shape[1]
    total = mine_ref[...] + swap_pairs(his_ref, part)
    low = total[:, units : units + rank].astype(BF16)
    pick = pick_ref[...]
    up = jnp.dot(up_ref[...], pick, preferred_element_type=F32).astype(BF16)
    cot = jnp.concatenate(
        [a_ref[...], next_b_ref[...], prev_a_ref[...], b_ref[...]], axis=0
    )
    cot = jnp.dot(cot, pick, preferred_element_type=F32)
    both = total[:, :units]
    gate = both + jnp.dot(low, up, preferred_element_type=F32)
    upper = pltpu.roll(both, units - n // 2, 1)
    s = jax.nn.sigmoid(gate)
    grad = (cot * upper * s * (1.0 + gate * (1.0 - s))).astype(BF16)
    low_grad = lax.dot_general(grad, up, NT, preferred_element_type=F32)
    ordered = lax.dot_general(grad, pick, NT, preferred_element_type=F32).astype(BF16)
    up_grad = lax.dot_general(low, ordered, TN, preferred_element_type=F32)
    group = 4 * part
    pieces = [up_grad[:, i * rank : (i + 1) * rank] for i in range(up_grad.shape[1] // rank)]
    plus_ref[:, :rank] = low_grad[:group]
    plus_ref[:, rank:] = jnp.concatenate(pieces, axis=0)
    minus_ref[...] = low_grad[group:]


def gate_stage(mine, his, cots, pick, up, n):
    rows = mine.shape[0]
    rank, hidden = up.shape
    vm = pl.BlockSpec(memory_space=pltpu.VMEM)
    return pl.pallas_call(
        functools.partial(gate_kernel, n=n, part=rows // 8, rank=rank),
        in_specs=[vm] * 8,
        out_specs=[vm, vm],
        out_shape=[
            jax.ShapeDtypeStruct((rows // 2, 2 * rank), F32),
            jax.ShapeDtypeStruct((rows // 2, rank), F32),
        ],
        compiler_params=params(24),
        cost_estimate=pl.CostEstimate(
            flops=2 * rows * hidden * (2 * hidden + 3 * rank),
            bytes_accessed=rows * hidden * 12,
            transcendentals=rows * hidden,
        ),
        name="gate_stage",
    )(mine, his, *cots, pick, up)


def down_kernel(xl_ref, *refs, block):
    x_refs, (plus_ref, minus_ref, from_next, from_prev, out_ref) = refs[:8], refs[8:]
    rank = minus_ref.shape[1]
    low = jnp.concatenate(
        [plus_ref[:, :rank] + from_next[...], minus_ref[...] + from_prev[:, :rank]], axis=0
    ).astype(BF16)
    up = plus_ref[:, rank:] + from_prev[:, rank:]
    up = jnp.concatenate(
        [up[i * rank : (i + 1) * rank] for i in range(up.shape[0] // rank)], axis=1
    )
    x = jnp.concatenate([r[0] for r in x_refs], axis=0)
    terms = lax.dot_general(low, x, TN, preferred_element_type=F32)
    lanes = out_ref.shape[-1]
    for i in range(4):
        row = jnp.concatenate([terms[:, i * block : (i + 1) * block], up], axis=1)
        for h in range(2):
            for g in range(rank // 8):
                piece = row[g * 8 : (g + 1) * 8, h * lanes : (h + 1) * lanes]
                out_ref[h * (rank // 8) + g, i] = piece.astype(BF16)


def down_terms(xs, xl, plus, minus, from_next, from_prev, ys, block):
    chunks, part, lanes = xs[0].shape
    per = chunks // 2
    group, rank = minus.shape
    hidden = group // rank * rank
    piece = (block + hidden) // 2
    x_spec = pl.BlockSpec((1, part, lanes), lambda k, v: (v[0] * per + k, 0, 0))
    both = pl.BlockSpec((group, 2 * rank), lambda k, v: (0, 0))
    single = pl.BlockSpec((group, rank), lambda k, v: (0, 0))
    return pl.pallas_call(
        functools.partial(down_kernel, block=block),
        grid_spec=pltpu.PrefetchScalarGridSpec(
            num_scalar_prefetch=1,
            grid=(per,),
            in_specs=[x_spec] * 8 + [both, single, single, both],
            out_specs=pl.BlockSpec((rank // 4, 4, 8, piece), lambda k, v: (0, k, 0, 0)),
        ),
        out_shape=jax.ShapeDtypeStruct((rank // 4, ys, 8, piece), BF16),
        compiler_params=params(60),
        cost_estimate=pl.CostEstimate(
            flops=2 * 2 * group * rank * ys * block,
            bytes_accessed=(2 * group + rank) * ys * block * 2,
            transcendentals=0,
        ),
        name="down_terms",
    )(xl, *xs, plus, minus, from_next, from_prev)


def chosen(condition):
    return condition.astype(BF16)


def cotangent_rows(grads, plan, counts, place):
    rows = grads.shape[0]
    lanes = lax.axis_size(WIDE)
    seg = rows // counts.shape[0]
    local = jnp.arange(rows, dtype=jnp.int32)
    slots = lax.dynamic_slice_in_dim(plan, place * rows, rows, 0)
    rank = jnp.sum((slots[None, :] < slots[:, None]).astype(jnp.int32), axis=1)
    owner = jnp.arange(plan.shape[0], dtype=jnp.int32) // rows
    held = plan[None, :] == (place * rows + local)[:, None]
    source = jnp.sum(jnp.where(held, owner[None, :], 0), axis=1)
    before = (source[None, :] == source[:, None]) & (local[None, :] < local[:, None])
    spot = source * (rows // lanes) + jnp.sum(before.astype(jnp.int32), axis=1)
    sent = jnp.dot(
        chosen(spot[None, :] == local[:, None]), grads, preferred_element_type=F32
    ).astype(BF16)
    back = exchange(sent, WIDE)
    live = local % seg < jnp.repeat(counts, seg, total_repeat_length=rows)
    pick = (rank[:, None] == local[None, :]) & live[:, None]
    return jnp.dot(chosen(pick), back, preferred_element_type=F32).astype(BF16)


def unit_order(slab, xl, ys, n, hidden):
    spans = slab.shape[0]
    per_span = hidden // spans
    units = n // (2 * spans)
    at = jnp.arange(ys * 2 * n, dtype=jnp.int32)
    y, core = at // (2 * n), at // n % 2
    gate, span, unit = at // (n // 2) % 2 == 0, at // units % spans, at % units
    k = ((y * 2 + xl) * 2 + core) * units + unit
    h = jnp.arange(hidden, dtype=jnp.int32)
    stored = jnp.repeat(slab, per_span, total_repeat_length=hidden)
    return chosen(
        gate[None, :]
        & (stored[:, None] == span[None, :])
        & ((h % per_span)[:, None] == k[None, :])
    )


def shards(x, grads, frozen, slab, down, up, counts, plan):
    ys = lax.axis_size("y")
    copies = lax.axis_size(DP)
    xl, core = lax.axis_index("xl"), lax.axis_index("core")
    rows, width = x.shape
    block, rank = down.shape
    hidden = up.shape[1]
    half = rows // 2
    n = 2 * frozen.shape[0] * frozen.shape[2]
    core_id = core.astype(jnp.int32).reshape(1)
    xl_id = xl.astype(jnp.int32).reshape(1)

    swapped = exchange(split_weights(frozen, ys, block), "core")
    chunks = swapped.shape[1]
    down_rows = down.T.reshape(4, rank // 4, block).transpose(1, 0, 2).reshape(rank // 4, 4 * block)
    near_down = shift(down_rows, "xl", 1)
    both_down = jnp.where(
        xl == 0,
        jnp.concatenate([down_rows, near_down], axis=0),
        jnp.concatenate([near_down, down_rows], axis=0),
    )
    sent = jnp.concatenate(
        [swapped.transpose(1, 0, 2, 3).reshape(chunks * 2 * n, 4 * block), both_down], axis=0
    )
    gathered = lax.all_gather(sent[None], "y", axis=0, tiled=True)

    parts = split_rows(x, core_id, ys, block)
    own_a, own_b, other_a, other_b, grads = lax.optimization_barrier((*parts, grads))
    next_own = shift(own_a, RING, 1)
    prev_own = shift(own_b, RING, -1)
    pair_a = shift(other_a, "core", 1)
    pair_b = shift(other_b, "core", 1)
    next_pair = shift(pair_a, RING, 1)
    prev_pair = shift(pair_b, RING, -1)
    cot = cotangent_rows(grads, plan[0], counts, lax.axis_index(WIDE))
    cot_pair = shift(cot, "core", 1)
    cot_a = jnp.concatenate([cot[:half], cot_pair[:half]], axis=0)
    cot_b = jnp.concatenate([cot[half:], cot_pair[half:]], axis=0)
    cot_a, cot_b, next_own, prev_own = lax.optimization_barrier(
        (cot_a, cot_b, next_own, prev_own)
    )
    cots = [cot_a, shift(cot_b, RING, -1), shift(cot_a, RING, 1), cot_b]

    gathered, cots, pick = lax.optimization_barrier(
        (gathered, cots, unit_order(slab, xl, ys, n, hidden))
    )
    xs = [own_a, pair_a, prev_own, prev_pair, next_own, next_pair, own_b, pair_b]
    mine = products(xs, gathered, n, rank, block)
    his = shift(mine, "core", 1)
    plus, minus = gate_stage(mine, his, cots, pick, up, n)
    from_prev = shift(plus, RING, 1)
    from_next = shift(minus, RING, -1)

    terms = down_terms(xs, xl_id, plus, minus, from_next, from_prev, ys, block)
    lanes = terms.shape[-1]
    terms = exchange(terms.reshape(copies * ys, 8, lanes), REPLICAS)
    total = terms.astype(F32).sum(0)
    full = exchange(jnp.tile(total[None], (copies, 1, 1)), DP)
    full = full.reshape(2, rank // 8, 8, lanes).transpose(1, 2, 0, 3).reshape(rank, 2 * lanes)
    return full[:, :block].T, full[:, block:]


def solution(mesh):
    dp, wide = mesh.devices.shape
    fine = Mesh(mesh.devices.reshape(dp // 2, 2, wide // 4, 2, 2), EVERY)
    placed = (
        P(EVERY, None),
        P(EVERY, None),
        P(None, None, WIDE, None),
        P(),
        P(WIDE, None),
        P(),
        P(EVERY),
        P(DP, None),
    )
    return jax.shard_map(
        shards, mesh=fine, in_specs=placed, out_specs=(P(WIDE, None), P()), check_vma=False
    )
```

```python
import functools

import jax
import jax.numpy as jnp
from jax import lax
from jax.experimental import pallas as pl
from jax.experimental.pallas import tpu as pltpu
from jax.sharding import Mesh
from jax.sharding import PartitionSpec as P

F32 = jnp.float32
BF16 = jnp.bfloat16
DP = ("z", "xh")
WIDE = ("y", "xl", "core")
RING = ("xh", "xl")
EVERY = ("z", "xh", "y", "xl", "core")
MIB = 1024 * 1024
NT = (((1,), (1,)), ((), ()))
TN = (((0,), (0,)), ((), ()))


def shift(array, axes, step):
    size = lax.axis_size(axes)
    return lax.ppermute(array, axes, [(i, (i + step) % size) for i in range(size)])


def exchange(array, axes):
    return lax.all_to_all(array, axes, split_axis=0, concat_axis=0, tiled=True)


def params(mib):
    return pltpu.CompilerParams(vmem_limit_bytes=mib * MIB)


def split_rows_kernel(core_ref, x_ref, own_a, own_b, other_a, other_b, *, block):
    core = core_ref[0]
    half = x_ref.shape[0] // 2
    for xl in range(2):
        mine = pl.multiple_of(xl * 2 * block + core * block, block)
        his = pl.multiple_of(xl * 2 * block + (1 - core) * block, block)
        own_a[xl, 0] = x_ref[:half, pl.ds(mine, block)]
        own_b[xl, 0] = x_ref[half:, pl.ds(mine, block)]
        other_a[xl, 0] = x_ref[:half, pl.ds(his, block)]
        other_b[xl, 0] = x_ref[half:, pl.ds(his, block)]


def split_rows(x, core, ys, block):
    rows, width = x.shape
    half = rows // 2
    shape = jax.ShapeDtypeStruct((2, ys // 4, half, 4 * block), BF16)
    spec = pl.BlockSpec((2, 1, half, block), lambda y, c: (0, y // 4, 0, y % 4))
    parts = pl.pallas_call(
        functools.partial(split_rows_kernel, block=block),
        grid_spec=pltpu.PrefetchScalarGridSpec(
            num_scalar_prefetch=1,
            grid=(ys,),
            in_specs=[pl.BlockSpec((rows, 4 * block), lambda y, c: (0, y))],
            out_specs=[spec] * 4,
        ),
        out_shape=[shape] * 4,
        compiler_params=params(24),
        cost_estimate=pl.CostEstimate(flops=0, bytes_accessed=rows * width * 4, transcendentals=0),
        name="split_rows",
    )(core, x)
    return [part.reshape(2 * (ys // 4), half, 4 * block) for part in parts]


def split_weights_kernel(w_ref, out_ref, *, block):
    spans, _, units, _ = w_ref.shape
    rows = jnp.concatenate(
        [w_ref[s, j].astype(F32) for j in range(2) for s in range(spans)], axis=0
    ).astype(BF16)
    for parity in range(2):
        for xl in range(2):
            for y in range(4):
                at = ((y * 2 + xl) * 2 + parity) * block
                out_ref[parity, xl, 0, :, y * block : (y + 1) * block] = rows[:, at : at + block]


def split_weights(w, ys, block):
    spans, _, units, width = w.shape
    n = 2 * spans * units
    out = pl.pallas_call(
        functools.partial(split_weights_kernel, block=block),
        grid=(ys // 4,),
        in_specs=[pl.BlockSpec((spans, 2, units, 16 * block), lambda y: (0, 0, 0, y))],
        out_specs=pl.BlockSpec((2, 2, 1, n, 4 * block), lambda y: (0, 0, y, 0, 0)),
        out_shape=jax.ShapeDtypeStruct((2, 2, ys // 4, n, 4 * block), BF16),
        compiler_params=params(24),
        cost_estimate=pl.CostEstimate(flops=0, bytes_accessed=w.size * 4, transcendentals=0),
        name="split_weights",
    )(w)
    return out.reshape(2, 2 * (ys // 4), n, 4 * block)


def products_kernel(*refs, block, rank, n):
    x_refs, (g_ref, out_ref, w_ref, down_ref, sems) = refs[:8], refs[8:]
    chunks = x_refs[0].shape[0]
    ys = g_ref.shape[0]
    copies = [
        pltpu.make_async_copy(g_ref.at[:, 2 * chunks * n :, :], down_ref, sems.at[chunks])
    ] + [
        pltpu.make_async_copy(
            g_ref.at[:, 2 * k * n : 2 * (k + 1) * n, :], w_ref.at[k], sems.at[k]
        )
        for k in range(chunks)
    ]
    for copy in copies:
        copy.start()
    copies[0].wait()
    units = ys * 2 * n
    part = rank // 4
    wide = low = None
    for k in range(chunks):
        copies[k + 1].wait()
        x = jnp.concatenate([r[k] for r in x_refs], axis=0)
        w = w_ref[k].reshape(units, -1)
        xl, first = divmod(k, chunks // 2)
        down = jnp.concatenate(
            [
                jnp.concatenate(
                    [
                        down_ref[
                            first * 4 + y,
                            xl * part : (xl + 1) * part,
                            t * block : (t + 1) * block,
                        ]
                        for t in range(4)
                    ],
                    axis=0,
                )
                for y in range(4)
            ],
            axis=1,
        )
        more_wide = lax.dot_general(x, w, NT, preferred_element_type=F32)
        more_low = lax.dot_general(x, down, NT, preferred_element_type=F32)
        wide = more_wide if wide is None else wide + more_wide
        low = more_low if low is None else low + more_low
    out_ref[:, :units] = wide
    out_ref[:, units : units + rank] = low
    out_ref[:, units + rank :] = jnp.zeros_like(out_ref[:, units + rank :])


def products(xs, gathered, n, rank, block):
    chunks, part, lanes = xs[0].shape
    ys = gathered.shape[0]
    units = ys * 2 * n
    columns = units + pl.cdiv(rank, 128) * 128
    vm = pl.BlockSpec(memory_space=pltpu.VMEM)
    return pl.pallas_call(
        functools.partial(products_kernel, block=block, rank=rank, n=n),
        in_specs=[vm] * 8 + [pl.BlockSpec(memory_space=pltpu.HBM)],
        out_specs=vm,
        out_shape=jax.ShapeDtypeStruct((8 * part, columns), F32),
        scratch_shapes=[
            pltpu.VMEM((chunks, ys, 2 * n, lanes), BF16),
            pltpu.VMEM((ys, rank // 2, lanes), BF16),
            pltpu.SemaphoreType.DMA((chunks + 1,)),
        ],
        compiler_params=params(51),
        cost_estimate=pl.CostEstimate(
            flops=2 * 8 * part * chunks * lanes * (units + rank),
            bytes_accessed=(8 * part + units + rank) * chunks * lanes * 2,
            transcendentals=0,
        ),
        name="products",
    )(*xs, gathered)


def swap_pairs(ref, part):
    return jnp.concatenate(
        [ref[(i ^ 1) * part : ((i ^ 1) + 1) * part] for i in range(8)], axis=0
    )


def gate_kernel(mine_ref, his_ref, a_ref, next_b_ref, prev_a_ref, b_ref, pick_ref, up_ref,
                plus_ref, minus_ref, *, n, part, rank):
    units = pick_ref.shape[1]
    total = mine_ref[...] + swap_pairs(his_ref, part)
    low = total[:, units : units + rank].astype(BF16)
    pick = pick_ref[...]
    up = jnp.dot(up_ref[...], pick, preferred_element_type=F32).astype(BF16)
    cot = jnp.concatenate(
        [a_ref[...], next_b_ref[...], prev_a_ref[...], b_ref[...]], axis=0
    )
    cot = jnp.dot(cot, pick, preferred_element_type=F32)
    both = total[:, :units]
    gate = both + jnp.dot(low, up, preferred_element_type=F32)
    upper = pltpu.roll(both, units - n // 2, 1)
    s = jax.nn.sigmoid(gate)
    grad = (cot * upper * s * (1.0 + gate * (1.0 - s))).astype(BF16)
    low_grad = lax.dot_general(grad, up, NT, preferred_element_type=F32)
    ordered = lax.dot_general(grad, pick, NT, preferred_element_type=F32).astype(BF16)
    up_grad = lax.dot_general(low, ordered, TN, preferred_element_type=F32)
    group = 4 * part
    pieces = [up_grad[:, i * rank : (i + 1) * rank] for i in range(up_grad.shape[1] // rank)]
    plus_ref[:, :rank] = low_grad[:group]
    plus_ref[:, rank:] = jnp.concatenate(pieces, axis=0)
    minus_ref[...] = low_grad[group:]


def gate_stage(mine, his, cots, pick, up, n):
    rows = mine.shape[0]
    rank, hidden = up.shape
    vm = pl.BlockSpec(memory_space=pltpu.VMEM)
    return pl.pallas_call(
        functools.partial(gate_kernel, n=n, part=rows // 8, rank=rank),
        in_specs=[vm] * 8,
        out_specs=[vm, vm],
        out_shape=[
            jax.ShapeDtypeStruct((rows // 2, 2 * rank), F32),
            jax.ShapeDtypeStruct((rows // 2, rank), F32),
        ],
        compiler_params=params(24),
        cost_estimate=pl.CostEstimate(
            flops=2 * rows * hidden * (2 * hidden + 3 * rank),
            bytes_accessed=rows * hidden * 12,
            transcendentals=rows * hidden,
        ),
        name="gate_stage",
    )(mine, his, *cots, pick, up)


def down_kernel(xl_ref, *refs, block):
    x_refs, (plus_ref, minus_ref, from_next, from_prev, out_ref) = refs[:8], refs[8:]
    rank = minus_ref.shape[1]
    low = jnp.concatenate(
        [plus_ref[:, :rank] + from_next[...], minus_ref[...] + from_prev[:, :rank]], axis=0
    ).astype(BF16)
    up = plus_ref[:, rank:] + from_prev[:, rank:]
    up = jnp.concatenate(
        [up[i * rank : (i + 1) * rank] for i in range(up.shape[0] // rank)], axis=1
    )
    per = x_refs[0].shape[0] // 2
    for k in range(per):
        x = jnp.concatenate([r[xl_ref[0] * per + k] for r in x_refs], axis=0)
        terms = lax.dot_general(low, x, TN, preferred_element_type=F32)
        for i in range(4):
            row = jnp.concatenate([terms[:, i * block : (i + 1) * block], up], axis=1)
            for g in range(rank // 8):
                out_ref[g, k * 4 + i] = row[g * 8 : (g + 1) * 8].astype(BF16)


def down_terms(xs, xl, plus, minus, from_next, from_prev, ys, block):
    group, rank = minus.shape
    hidden = group // rank * rank
    vm = pl.BlockSpec(memory_space=pltpu.VMEM)
    return pl.pallas_call(
        functools.partial(down_kernel, block=block),
        in_specs=[pl.BlockSpec(memory_space=pltpu.SMEM)] + [vm] * 12,
        out_specs=vm,
        out_shape=jax.ShapeDtypeStruct((rank // 8, ys, 8, block + hidden), BF16),
        compiler_params=params(24),
        cost_estimate=pl.CostEstimate(
            flops=2 * 2 * group * rank * ys * block,
            bytes_accessed=(2 * group + rank) * ys * block * 2,
            transcendentals=0,
        ),
        name="down_terms",
    )(xl, *xs, plus, minus, from_next, from_prev)


def chosen(condition):
    return condition.astype(BF16)


def cotangent_rows(grads, plan, counts, place):
    rows = grads.shape[0]
    lanes = lax.axis_size(WIDE)
    seg = rows // counts.shape[0]
    local = jnp.arange(rows, dtype=jnp.int32)
    slots = lax.dynamic_slice_in_dim(plan, place * rows, rows, 0)
    rank = jnp.sum((slots[None, :] < slots[:, None]).astype(jnp.int32), axis=1)
    owner = jnp.arange(plan.shape[0], dtype=jnp.int32) // rows
    held = plan[None, :] == (place * rows + local)[:, None]
    source = jnp.sum(jnp.where(held, owner[None, :], 0), axis=1)
    before = (source[None, :] == source[:, None]) & (local[None, :] < local[:, None])
    spot = source * (rows // lanes) + jnp.sum(before.astype(jnp.int32), axis=1)
    sent = jnp.dot(
        chosen(spot[None, :] == local[:, None]), grads, preferred_element_type=F32
    ).astype(BF16)
    back = exchange(sent, WIDE)
    live = local % seg < jnp.repeat(counts, seg, total_repeat_length=rows)
    pick = (rank[:, None] == local[None, :]) & live[:, None]
    return jnp.dot(chosen(pick), back, preferred_element_type=F32).astype(BF16)


def unit_order(slab, xl, ys, n, hidden):
    spans = slab.shape[0]
    per_span = hidden // spans
    units = n // (2 * spans)
    at = jnp.arange(ys * 2 * n, dtype=jnp.int32)
    y, core = at // (2 * n), at // n % 2
    gate, span, unit = at // (n // 2) % 2 == 0, at // units % spans, at % units
    k = ((y * 2 + xl) * 2 + core) * units + unit
    h = jnp.arange(hidden, dtype=jnp.int32)
    stored = jnp.repeat(slab, per_span, total_repeat_length=hidden)
    return chosen(
        gate[None, :]
        & (stored[:, None] == span[None, :])
        & ((h % per_span)[:, None] == k[None, :])
    )


def shards(x, grads, frozen, slab, down, up, counts, plan):
    ys = lax.axis_size("y")
    copies = lax.axis_size(DP)
    xl, core = lax.axis_index("xl"), lax.axis_index("core")
    rows, width = x.shape
    block, rank = down.shape
    hidden = up.shape[1]
    half = rows // 2
    n = 2 * frozen.shape[0] * frozen.shape[2]
    core_id = core.astype(jnp.int32).reshape(1)
    xl_id = xl.astype(jnp.int32).reshape(1)

    swapped = exchange(split_weights(frozen, ys, block), "core")
    chunks = swapped.shape[1]
    down_rows = down.T.reshape(4, rank // 4, block).transpose(1, 0, 2).reshape(rank // 4, 4 * block)
    near_down = shift(down_rows, "xl", 1)
    both_down = jnp.where(
        xl == 0,
        jnp.concatenate([down_rows, near_down], axis=0),
        jnp.concatenate([near_down, down_rows], axis=0),
    )
    sent = jnp.concatenate(
        [swapped.transpose(1, 0, 2, 3).reshape(chunks * 2 * n, 4 * block), both_down], axis=0
    )
    gathered = lax.all_gather(sent[None], "y", axis=0, tiled=True)

    own_a, own_b, other_a, other_b = split_rows(x, core_id, ys, block)
    next_own = shift(own_a, RING, 1)
    prev_own = shift(own_b, RING, -1)
    pair_a = shift(other_a, "core", 1)
    pair_b = shift(other_b, "core", 1)
    pair_a, pair_b, grads = lax.optimization_barrier((pair_a, pair_b, grads))
    next_pair = shift(pair_a, RING, 1)
    prev_pair = shift(pair_b, RING, -1)
    cot = cotangent_rows(grads, plan[0], counts, lax.axis_index(WIDE))
    cot_pair = shift(cot, "core", 1)
    cot_a = jnp.concatenate([cot[:half], cot_pair[:half]], axis=0)
    cot_b = jnp.concatenate([cot[half:], cot_pair[half:]], axis=0)
    cot_a, cot_b, next_own, prev_own = lax.optimization_barrier(
        (cot_a, cot_b, next_own, prev_own)
    )
    cots = [cot_a, shift(cot_b, RING, -1), shift(cot_a, RING, 1), cot_b]

    gathered, cots, pick = lax.optimization_barrier(
        (gathered, cots, unit_order(slab, xl, ys, n, hidden))
    )
    xs = [own_a, pair_a, prev_own, prev_pair, next_own, next_pair, own_b, pair_b]
    mine = products(xs, gathered, n, rank, block)
    his = shift(mine, "core", 1)
    plus, minus = gate_stage(mine, his, cots, pick, up, n)
    from_prev = shift(plus, RING, 1)
    from_next = shift(minus, RING, -1)

    terms = down_terms(xs, xl_id, plus, minus, from_next, from_prev, ys, block)
    lanes = terms.shape[-1]
    terms = exchange(terms.reshape(-1, 8, lanes), ("z", "y"))
    total = terms.astype(F32).sum(0).astype(BF16)
    full = exchange(jnp.tile(total[None], (copies, 1, 1)), DP)
    full = full.astype(F32).reshape(rank // 8, -1, 8, lanes).sum(1).reshape(rank, lanes)
    return full[:, :block].T, full[:, block:]


def solution(mesh):
    dp, wide = mesh.devices.shape
    fine = Mesh(mesh.devices.reshape(dp // 2, 2, wide // 4, 2, 2), EVERY)
    placed = (
        P(EVERY, None),
        P(EVERY, None),
        P(None, None, WIDE, None),
        P(),
        P(WIDE, None),
        P(),
        P(EVERY),
        P(DP, None),
    )
    return jax.shard_map(
        shards, mesh=fine, in_specs=placed, out_specs=(P(WIDE, None), P()), check_vma=False
    )
```

```python
import functools

import jax
import jax.numpy as jnp
from jax import lax
from jax.experimental import pallas as pl
from jax.experimental.pallas import tpu as pltpu
from jax.sharding import Mesh
from jax.sharding import PartitionSpec as P

F32 = jnp.float32
BF16 = jnp.bfloat16
DP = ("z", "xh")
WIDE = ("y", "xl", "core")
RING = ("xh", "xl")
EVERY = ("z", "xh", "y", "xl", "core")
MIB = 1024 * 1024
NT = (((1,), (1,)), ((), ()))
TN = (((0,), (0,)), ((), ()))


def shift(array, axes, step):
    size = lax.axis_size(axes)
    return lax.ppermute(array, axes, [(i, (i + step) % size) for i in range(size)])


def exchange(array, axes):
    return lax.all_to_all(array, axes, split_axis=0, concat_axis=0, tiled=True)


def params(mib):
    return pltpu.CompilerParams(vmem_limit_bytes=mib * MIB)


def split_rows_kernel(core_ref, x_ref, own_a, own_b, other_a, other_b, *, block):
    core = core_ref[0]
    half = x_ref.shape[0] // 2
    for xl in range(2):
        mine = pl.multiple_of(xl * 2 * block + core * block, block)
        his = pl.multiple_of(xl * 2 * block + (1 - core) * block, block)
        own_a[xl, 0] = x_ref[:half, pl.ds(mine, block)]
        own_b[xl, 0] = x_ref[half:, pl.ds(mine, block)]
        other_a[xl, 0] = x_ref[:half, pl.ds(his, block)]
        other_b[xl, 0] = x_ref[half:, pl.ds(his, block)]


def split_rows(x, core, ys, block):
    rows, width = x.shape
    half = rows // 2
    shape = jax.ShapeDtypeStruct((2, ys // 4, half, 4 * block), BF16)
    spec = pl.BlockSpec((2, 1, half, block), lambda y, c: (0, y // 4, 0, y % 4))
    parts = pl.pallas_call(
        functools.partial(split_rows_kernel, block=block),
        grid_spec=pltpu.PrefetchScalarGridSpec(
            num_scalar_prefetch=1,
            grid=(ys,),
            in_specs=[pl.BlockSpec((rows, 4 * block), lambda y, c: (0, y))],
            out_specs=[spec] * 4,
        ),
        out_shape=[shape] * 4,
        compiler_params=params(24),
        cost_estimate=pl.CostEstimate(flops=0, bytes_accessed=rows * width * 4, transcendentals=0),
        name="split_rows",
    )(core, x)
    return [part.reshape(2 * (ys // 4), half, 4 * block) for part in parts]


def split_weights_kernel(w_ref, out_ref, *, block):
    spans, _, units, _ = w_ref.shape
    rows = jnp.concatenate(
        [w_ref[s, j].astype(F32) for j in range(2) for s in range(spans)], axis=0
    ).astype(BF16)
    for parity in range(2):
        for xl in range(2):
            for y in range(4):
                at = ((y * 2 + xl) * 2 + parity) * block
                out_ref[parity, xl, 0, :, y * block : (y + 1) * block] = rows[:, at : at + block]


def split_weights(w, ys, block):
    spans, _, units, width = w.shape
    n = 2 * spans * units
    out = pl.pallas_call(
        functools.partial(split_weights_kernel, block=block),
        grid=(ys // 4,),
        in_specs=[pl.BlockSpec((spans, 2, units, 16 * block), lambda y: (0, 0, 0, y))],
        out_specs=pl.BlockSpec((2, 2, 1, n, 4 * block), lambda y: (0, 0, y, 0, 0)),
        out_shape=jax.ShapeDtypeStruct((2, 2, ys // 4, n, 4 * block), BF16),
        compiler_params=params(24),
        cost_estimate=pl.CostEstimate(flops=0, bytes_accessed=w.size * 4, transcendentals=0),
        name="split_weights",
    )(w)
    return out.reshape(2, 2 * (ys // 4), n, 4 * block)


def products_kernel(*refs, block, rank, n):
    x_refs, (g_ref, out_ref, w_ref, down_ref, sems) = refs[:8], refs[8:]
    chunks = x_refs[0].shape[0]
    ys = g_ref.shape[0]
    copies = [
        pltpu.make_async_copy(g_ref.at[:, 2 * chunks * n :, :], down_ref, sems.at[chunks])
    ] + [
        pltpu.make_async_copy(
            g_ref.at[:, 2 * k * n : 2 * (k + 1) * n, :], w_ref.at[k], sems.at[k]
        )
        for k in range(chunks)
    ]
    for copy in copies:
        copy.start()
    copies[0].wait()
    units = ys * 2 * n
    part = rank // 4
    total = None
    for k in range(chunks):
        x = jnp.concatenate([r[k] for r in x_refs], axis=0)
        xl, first = divmod(k, chunks // 2)
        down = jnp.concatenate(
            [
                jnp.concatenate(
                    [
                        down_ref[
                            first * 4 + y,
                            xl * part : (xl + 1) * part,
                            t * block : (t + 1) * block,
                        ]
                        for t in range(4)
                    ],
                    axis=0,
                )
                for y in range(4)
            ],
            axis=1,
        )
        copies[k + 1].wait()
        w = jnp.concatenate([w_ref[k].reshape(units, -1), down], axis=0)
        more = lax.dot_general(w, x, NT, preferred_element_type=F32)
        total = more if total is None else total + more
    out_ref[:, : units + rank] = total.T
    out_ref[:, units + rank :] = jnp.zeros_like(out_ref[:, units + rank :])


def products(xs, gathered, n, rank, block):
    chunks, part, lanes = xs[0].shape
    ys = gathered.shape[0]
    units = ys * 2 * n
    columns = units + pl.cdiv(rank, 128) * 128
    vm = pl.BlockSpec(memory_space=pltpu.VMEM)
    return pl.pallas_call(
        functools.partial(products_kernel, block=block, rank=rank, n=n),
        in_specs=[vm] * 8 + [pl.BlockSpec(memory_space=pltpu.HBM)],
        out_specs=vm,
        out_shape=jax.ShapeDtypeStruct((8 * part, columns), F32),
        scratch_shapes=[
            pltpu.VMEM((chunks, ys, 2 * n, lanes), BF16),
            pltpu.VMEM((ys, rank // 2, lanes), BF16),
            pltpu.SemaphoreType.DMA((chunks + 1,)),
        ],
        compiler_params=params(51),
        cost_estimate=pl.CostEstimate(
            flops=2 * 8 * part * chunks * lanes * (units + rank),
            bytes_accessed=(8 * part + units + rank) * chunks * lanes * 2,
            transcendentals=0,
        ),
        name="products",
    )(*xs, gathered)


def swap_pairs(ref, part):
    return jnp.concatenate(
        [ref[(i ^ 1) * part : ((i ^ 1) + 1) * part] for i in range(8)], axis=0
    )


def gate_kernel(mine_ref, his_ref, a_ref, next_b_ref, prev_a_ref, b_ref, pick_ref, up_ref,
                plus_ref, minus_ref, *, n, part, rank):
    units = pick_ref.shape[1]
    total = mine_ref[...] + swap_pairs(his_ref, part)
    low = total[:, units : units + rank].astype(BF16)
    pick = pick_ref[...]
    up = jnp.dot(up_ref[...], pick, preferred_element_type=F32).astype(BF16)
    cot = jnp.concatenate(
        [a_ref[...], next_b_ref[...], prev_a_ref[...], b_ref[...]], axis=0
    )
    cot = jnp.dot(cot, pick, preferred_element_type=F32)
    both = total[:, :units]
    gate = both + jnp.dot(low, up, preferred_element_type=F32)
    upper = pltpu.roll(both, units - n // 2, 1)
    s = jax.nn.sigmoid(gate)
    grad = (cot * upper * s * (1.0 + gate * (1.0 - s))).astype(BF16)
    low_grad = lax.dot_general(grad, up, NT, preferred_element_type=F32)
    ordered = lax.dot_general(grad, pick, NT, preferred_element_type=F32).astype(BF16)
    up_grad = lax.dot_general(low, ordered, TN, preferred_element_type=F32)
    group = 4 * part
    pieces = [up_grad[:, i * rank : (i + 1) * rank] for i in range(up_grad.shape[1] // rank)]
    plus_ref[:, :rank] = low_grad[:group]
    plus_ref[:, rank:] = jnp.concatenate(pieces, axis=0)
    minus_ref[...] = low_grad[group:]


def gate_stage(mine, his, cots, pick, up, n):
    rows = mine.shape[0]
    rank, hidden = up.shape
    vm = pl.BlockSpec(memory_space=pltpu.VMEM)
    return pl.pallas_call(
        functools.partial(gate_kernel, n=n, part=rows // 8, rank=rank),
        in_specs=[vm] * 8,
        out_specs=[vm, vm],
        out_shape=[
            jax.ShapeDtypeStruct((rows // 2, 2 * rank), F32),
            jax.ShapeDtypeStruct((rows // 2, rank), F32),
        ],
        compiler_params=params(24),
        cost_estimate=pl.CostEstimate(
            flops=2 * rows * hidden * (2 * hidden + 3 * rank),
            bytes_accessed=rows * hidden * 12,
            transcendentals=rows * hidden,
        ),
        name="gate_stage",
    )(mine, his, *cots, pick, up)


def down_kernel(xl_ref, *refs, block):
    x_refs, (plus_ref, minus_ref, from_next, from_prev, out_ref) = refs[:8], refs[8:]
    rank = minus_ref.shape[1]
    low = jnp.concatenate(
        [plus_ref[:, :rank] + from_next[...], minus_ref[...] + from_prev[:, :rank]], axis=0
    ).astype(BF16)
    up = plus_ref[:, rank:] + from_prev[:, rank:]
    up = jnp.concatenate(
        [up[i * rank : (i + 1) * rank] for i in range(up.shape[0] // rank)], axis=1
    )
    per = x_refs[0].shape[0] // 2
    for k in range(per):
        x = jnp.concatenate([r[xl_ref[0] * per + k] for r in x_refs], axis=0)
        terms = lax.dot_general(low, x, TN, preferred_element_type=F32)
        for i in range(4):
            row = jnp.concatenate([terms[:, i * block : (i + 1) * block], up], axis=1)
            for g in range(rank // 8):
                out_ref[g, k * 4 + i] = row[g * 8 : (g + 1) * 8].astype(BF16)


def down_terms(xs, xl, plus, minus, from_next, from_prev, ys, block):
    group, rank = minus.shape
    hidden = group // rank * rank
    vm = pl.BlockSpec(memory_space=pltpu.VMEM)
    return pl.pallas_call(
        functools.partial(down_kernel, block=block),
        in_specs=[pl.BlockSpec(memory_space=pltpu.SMEM)] + [vm] * 12,
        out_specs=vm,
        out_shape=jax.ShapeDtypeStruct((rank // 8, ys, 8, block + hidden), BF16),
        compiler_params=params(24),
        cost_estimate=pl.CostEstimate(
            flops=2 * 2 * group * rank * ys * block,
            bytes_accessed=(2 * group + rank) * ys * block * 2,
            transcendentals=0,
        ),
        name="down_terms",
    )(xl, *xs, plus, minus, from_next, from_prev)


def chosen(condition):
    return condition.astype(BF16)


def cotangent_rows(grads, plan, counts, place):
    rows = grads.shape[0]
    lanes = lax.axis_size(WIDE)
    seg = rows // counts.shape[0]
    local = jnp.arange(rows, dtype=jnp.int32)
    slots = lax.dynamic_slice_in_dim(plan, place * rows, rows, 0)
    rank = jnp.sum((slots[None, :] < slots[:, None]).astype(jnp.int32), axis=1)
    owner = jnp.arange(plan.shape[0], dtype=jnp.int32) // rows
    held = plan[None, :] == (place * rows + local)[:, None]
    source = jnp.sum(jnp.where(held, owner[None, :], 0), axis=1)
    before = (source[None, :] == source[:, None]) & (local[None, :] < local[:, None])
    spot = source * (rows // lanes) + jnp.sum(before.astype(jnp.int32), axis=1)
    sent = jnp.dot(
        chosen(spot[None, :] == local[:, None]), grads, preferred_element_type=F32
    ).astype(BF16)
    back = exchange(sent, WIDE)
    live = local % seg < jnp.repeat(counts, seg, total_repeat_length=rows)
    pick = (rank[:, None] == local[None, :]) & live[:, None]
    return jnp.dot(chosen(pick), back, preferred_element_type=F32).astype(BF16)


def unit_order(slab, xl, ys, n, hidden):
    spans = slab.shape[0]
    per_span = hidden // spans
    units = n // (2 * spans)
    at = jnp.arange(ys * 2 * n, dtype=jnp.int32)
    y, core = at // (2 * n), at // n % 2
    gate, span, unit = at // (n // 2) % 2 == 0, at // units % spans, at % units
    k = ((y * 2 + xl) * 2 + core) * units + unit
    h = jnp.arange(hidden, dtype=jnp.int32)
    stored = jnp.repeat(slab, per_span, total_repeat_length=hidden)
    return chosen(
        gate[None, :]
        & (stored[:, None] == span[None, :])
        & ((h % per_span)[:, None] == k[None, :])
    )


def shards(x, grads, frozen, slab, down, up, counts, plan):
    ys = lax.axis_size("y")
    copies = lax.axis_size(DP)
    xl, core = lax.axis_index("xl"), lax.axis_index("core")
    rows, width = x.shape
    block, rank = down.shape
    hidden = up.shape[1]
    half = rows // 2
    n = 2 * frozen.shape[0] * frozen.shape[2]
    core_id = core.astype(jnp.int32).reshape(1)
    xl_id = xl.astype(jnp.int32).reshape(1)

    swapped = exchange(split_weights(frozen, ys, block), "core")
    chunks = swapped.shape[1]
    down_rows = down.T.reshape(4, rank // 4, block).transpose(1, 0, 2).reshape(rank // 4, 4 * block)
    near_down = shift(down_rows, "xl", 1)
    both_down = jnp.where(
        xl == 0,
        jnp.concatenate([down_rows, near_down], axis=0),
        jnp.concatenate([near_down, down_rows], axis=0),
    )
    sent = jnp.concatenate(
        [swapped.transpose(1, 0, 2, 3).reshape(chunks * 2 * n, 4 * block), both_down], axis=0
    )
    gathered = lax.all_gather(sent[None], "y", axis=0, tiled=True)

    own_a, own_b, other_a, other_b = split_rows(x, core_id, ys, block)
    next_own = shift(own_a, RING, 1)
    prev_own = shift(own_b, RING, -1)
    pair_a = shift(other_a, "core", 1)
    pair_b = shift(other_b, "core", 1)
    pair_a, pair_b, grads = lax.optimization_barrier((pair_a, pair_b, grads))
    next_pair = shift(pair_a, RING, 1)
    prev_pair = shift(pair_b, RING, -1)
    cot = cotangent_rows(grads, plan[0], counts, lax.axis_index(WIDE))
    cot_pair = shift(cot, "core", 1)
    cot_a = jnp.concatenate([cot[:half], cot_pair[:half]], axis=0)
    cot_b = jnp.concatenate([cot[half:], cot_pair[half:]], axis=0)
    cot_a, cot_b, next_own, prev_own = lax.optimization_barrier(
        (cot_a, cot_b, next_own, prev_own)
    )
    cots = [cot_a, shift(cot_b, RING, -1), shift(cot_a, RING, 1), cot_b]

    gathered, cots, pick = lax.optimization_barrier(
        (gathered, cots, unit_order(slab, xl, ys, n, hidden))
    )
    xs = [own_a, pair_a, prev_own, prev_pair, next_own, next_pair, own_b, pair_b]
    mine = products(xs, gathered, n, rank, block)
    his = shift(mine, "core", 1)
    plus, minus = gate_stage(mine, his, cots, pick, up, n)
    from_prev = shift(plus, RING, 1)
    from_next = shift(minus, RING, -1)

    terms = down_terms(xs, xl_id, plus, minus, from_next, from_prev, ys, block)
    lanes = terms.shape[-1]
    terms = exchange(terms.reshape(-1, 8, lanes), ("z", "y"))
    total = terms.astype(F32).sum(0).astype(BF16)
    full = exchange(jnp.tile(total[None], (copies, 1, 1)), DP)
    full = full.astype(F32).reshape(rank // 8, -1, 8, lanes).sum(1).reshape(rank, lanes)
    return full[:, :block].T, full[:, block:]


def solution(mesh):
    dp, wide = mesh.devices.shape
    fine = Mesh(mesh.devices.reshape(dp // 2, 2, wide // 4, 2, 2), EVERY)
    placed = (
        P(EVERY, None),
        P(EVERY, None),
        P(None, None, WIDE, None),
        P(),
        P(WIDE, None),
        P(),
        P(EVERY),
        P(DP, None),
    )
    return jax.shard_map(
        shards, mesh=fine, in_specs=placed, out_specs=(P(WIDE, None), P()), check_vma=False
    )
```

```python
import functools

import jax
import jax.numpy as jnp
from jax import lax
from jax.experimental import pallas as pl
from jax.experimental.pallas import tpu as pltpu
from jax.sharding import Mesh
from jax.sharding import PartitionSpec as P

F32 = jnp.float32
BF16 = jnp.bfloat16
DP = ("z", "xh")
WIDE = ("y", "xl", "core")
RING = ("xh", "xl")
EVERY = ("z", "xh", "y", "xl", "core")
MIB = 1024 * 1024
NT = (((1,), (1,)), ((), ()))
TN = (((0,), (0,)), ((), ()))


def shift(array, axes, step):
    size = lax.axis_size(axes)
    return lax.ppermute(array, axes, [(i, (i + step) % size) for i in range(size)])


def exchange(array, axes):
    return lax.all_to_all(array, axes, split_axis=0, concat_axis=0, tiled=True)


def params(mib):
    return pltpu.CompilerParams(vmem_limit_bytes=mib * MIB)


def split_rows_kernel(core_ref, x_ref, own_a, own_b, other_a, other_b, *, block):
    core = core_ref[0]
    half = x_ref.shape[0] // 2
    for xl in range(2):
        mine = pl.multiple_of(xl * 2 * block + core * block, block)
        his = pl.multiple_of(xl * 2 * block + (1 - core) * block, block)
        own_a[xl, 0] = x_ref[:half, pl.ds(mine, block)]
        own_b[xl, 0] = x_ref[half:, pl.ds(mine, block)]
        other_a[xl, 0] = x_ref[:half, pl.ds(his, block)]
        other_b[xl, 0] = x_ref[half:, pl.ds(his, block)]


def split_rows(x, core, ys, block):
    rows, width = x.shape
    half = rows // 2
    shape = jax.ShapeDtypeStruct((2, ys // 4, half, 4 * block), BF16)
    spec = pl.BlockSpec((2, 1, half, block), lambda y, c: (0, y // 4, 0, y % 4))
    parts = pl.pallas_call(
        functools.partial(split_rows_kernel, block=block),
        grid_spec=pltpu.PrefetchScalarGridSpec(
            num_scalar_prefetch=1,
            grid=(ys,),
            in_specs=[pl.BlockSpec((rows, 4 * block), lambda y, c: (0, y))],
            out_specs=[spec] * 4,
        ),
        out_shape=[shape] * 4,
        compiler_params=params(24),
        cost_estimate=pl.CostEstimate(flops=0, bytes_accessed=rows * width * 4, transcendentals=0),
        name="split_rows",
    )(core, x)
    return [part.reshape(2 * (ys // 4), half, 4 * block) for part in parts]


def split_weights_kernel(w_ref, out_ref, *, block):
    spans, _, units, _ = w_ref.shape
    rows = jnp.concatenate(
        [w_ref[s, j].astype(F32) for j in range(2) for s in range(spans)], axis=0
    ).astype(BF16)
    for parity in range(2):
        for xl in range(2):
            for y in range(4):
                at = ((y * 2 + xl) * 2 + parity) * block
                out_ref[parity, xl, 0, :, y * block : (y + 1) * block] = rows[:, at : at + block]


def split_weights(w, ys, block):
    spans, _, units, width = w.shape
    n = 2 * spans * units
    out = pl.pallas_call(
        functools.partial(split_weights_kernel, block=block),
        grid=(ys // 4,),
        in_specs=[pl.BlockSpec((spans, 2, units, 16 * block), lambda y: (0, 0, 0, y))],
        out_specs=pl.BlockSpec((2, 2, 1, n, 4 * block), lambda y: (0, 0, y, 0, 0)),
        out_shape=jax.ShapeDtypeStruct((2, 2, ys // 4, n, 4 * block), BF16),
        compiler_params=params(24),
        cost_estimate=pl.CostEstimate(flops=0, bytes_accessed=w.size * 4, transcendentals=0),
        name="split_weights",
    )(w)
    return out.reshape(2, 2 * (ys // 4), n, 4 * block)


def products_kernel(*refs, block, rank, n):
    x_refs, (g_ref, out_ref, w_ref, down_ref, sems) = refs[:8], refs[8:]
    chunks = x_refs[0].shape[0]
    ys = g_ref.shape[0]
    copies = [
        pltpu.make_async_copy(g_ref.at[:, 2 * chunks * n :, :], down_ref, sems.at[chunks])
    ] + [
        pltpu.make_async_copy(
            g_ref.at[:, 2 * k * n : 2 * (k + 1) * n, :], w_ref.at[k], sems.at[k]
        )
        for k in range(chunks)
    ]
    for copy in copies:
        copy.start()
    copies[0].wait()
    units = ys * 2 * n
    part = rank // 4
    total = None
    for k in range(chunks):
        x = jnp.concatenate([r[k] for r in x_refs], axis=0)
        xl, first = divmod(k, chunks // 2)
        down = jnp.concatenate(
            [
                jnp.concatenate(
                    [
                        down_ref[
                            first * 4 + y,
                            xl * part : (xl + 1) * part,
                            t * block : (t + 1) * block,
                        ]
                        for t in range(4)
                    ],
                    axis=0,
                )
                for y in range(4)
            ],
            axis=1,
        )
        copies[k + 1].wait()
        w = jnp.concatenate([w_ref[k].reshape(units, -1), down], axis=0)
        more = lax.dot_general(w, x, NT, preferred_element_type=F32)
        total = more if total is None else total + more
    out_ref[:, : units + rank] = total.T
    out_ref[:, units + rank :] = jnp.zeros_like(out_ref[:, units + rank :])


def products(xs, gathered, n, rank, block):
    chunks, part, lanes = xs[0].shape
    ys = gathered.shape[0]
    units = ys * 2 * n
    columns = units + pl.cdiv(rank, 128) * 128
    vm = pl.BlockSpec(memory_space=pltpu.VMEM)
    return pl.pallas_call(
        functools.partial(products_kernel, block=block, rank=rank, n=n),
        in_specs=[vm] * 8 + [pl.BlockSpec(memory_space=pltpu.HBM)],
        out_specs=vm,
        out_shape=jax.ShapeDtypeStruct((8 * part, columns), F32),
        scratch_shapes=[
            pltpu.VMEM((chunks, ys, 2 * n, lanes), BF16),
            pltpu.VMEM((ys, rank // 2, lanes), BF16),
            pltpu.SemaphoreType.DMA((chunks + 1,)),
        ],
        compiler_params=params(49),
        cost_estimate=pl.CostEstimate(
            flops=2 * 8 * part * chunks * lanes * (units + rank),
            bytes_accessed=(8 * part + units + rank) * chunks * lanes * 2,
            transcendentals=0,
        ),
        name="products",
    )(*xs, gathered)


def swap_pairs(ref, part):
    return jnp.concatenate(
        [ref[(i ^ 1) * part : ((i ^ 1) + 1) * part] for i in range(8)], axis=0
    )


def gate_kernel(mine_ref, his_ref, a_ref, next_b_ref, prev_a_ref, b_ref, pick_ref, up_ref,
                plus_ref, minus_ref, *, n, part, rank):
    units = pick_ref.shape[1]
    total = mine_ref[...] + swap_pairs(his_ref, part)
    low = total[:, units : units + rank].astype(BF16)
    pick = pick_ref[...]
    up = jnp.dot(up_ref[...], pick, preferred_element_type=F32).astype(BF16)
    cot = jnp.concatenate(
        [a_ref[...], next_b_ref[...], prev_a_ref[...], b_ref[...]], axis=0
    )
    cot = jnp.dot(cot, pick, preferred_element_type=F32)
    both = total[:, :units]
    gate = both + jnp.dot(low, up, preferred_element_type=F32)
    upper = pltpu.roll(both, units - n // 2, 1)
    s = jax.nn.sigmoid(gate)
    grad = (cot * upper * s * (1.0 + gate * (1.0 - s))).astype(BF16)
    low_grad = lax.dot_general(grad, up, NT, preferred_element_type=F32)
    ordered = lax.dot_general(grad, pick, NT, preferred_element_type=F32).astype(BF16)
    up_grad = lax.dot_general(low, ordered, TN, preferred_element_type=F32)
    group = 4 * part
    pieces = [up_grad[:, i * rank : (i + 1) * rank] for i in range(up_grad.shape[1] // rank)]
    plus_ref[:, :rank] = low_grad[:group]
    plus_ref[:, rank:] = jnp.concatenate(pieces, axis=0)
    minus_ref[...] = low_grad[group:]


def gate_stage(mine, his, cots, pick, up, n):
    rows = mine.shape[0]
    rank, hidden = up.shape
    vm = pl.BlockSpec(memory_space=pltpu.VMEM)
    return pl.pallas_call(
        functools.partial(gate_kernel, n=n, part=rows // 8, rank=rank),
        in_specs=[vm] * 8,
        out_specs=[vm, vm],
        out_shape=[
            jax.ShapeDtypeStruct((rows // 2, 2 * rank), F32),
            jax.ShapeDtypeStruct((rows // 2, rank), F32),
        ],
        compiler_params=params(24),
        cost_estimate=pl.CostEstimate(
            flops=2 * rows * hidden * (2 * hidden + 3 * rank),
            bytes_accessed=rows * hidden * 12,
            transcendentals=rows * hidden,
        ),
        name="gate_stage",
    )(mine, his, *cots, pick, up)


def down_kernel(xl_ref, *refs, block):
    x_refs, (plus_ref, minus_ref, from_next, from_prev, out_ref) = refs[:8], refs[8:]
    rank = minus_ref.shape[1]
    low = jnp.concatenate(
        [plus_ref[:, :rank] + from_next[...], minus_ref[...] + from_prev[:, :rank]], axis=0
    ).astype(BF16)
    up = plus_ref[:, rank:] + from_prev[:, rank:]
    up = jnp.concatenate(
        [up[i * rank : (i + 1) * rank] for i in range(up.shape[0] // rank)], axis=1
    )
    per = x_refs[0].shape[0] // 2
    for k in range(per):
        x = jnp.concatenate([r[xl_ref[0] * per + k] for r in x_refs], axis=0)
        terms = lax.dot_general(low, x, TN, preferred_element_type=F32)
        for i in range(4):
            row = jnp.concatenate([terms[:, i * block : (i + 1) * block], up], axis=1)
            for g in range(rank // 8):
                out_ref[g, k * 4 + i] = row[g * 8 : (g + 1) * 8].astype(BF16)


def down_terms(xs, xl, plus, minus, from_next, from_prev, ys, block):
    group, rank = minus.shape
    hidden = group // rank * rank
    vm = pl.BlockSpec(memory_space=pltpu.VMEM)
    return pl.pallas_call(
        functools.partial(down_kernel, block=block),
        in_specs=[pl.BlockSpec(memory_space=pltpu.SMEM)] + [vm] * 12,
        out_specs=vm,
        out_shape=jax.ShapeDtypeStruct((rank // 8, ys, 8, block + hidden), BF16),
        compiler_params=params(24),
        cost_estimate=pl.CostEstimate(
            flops=2 * 2 * group * rank * ys * block,
            bytes_accessed=(2 * group + rank) * ys * block * 2,
            transcendentals=0,
        ),
        name="down_terms",
    )(xl, *xs, plus, minus, from_next, from_prev)


def chosen(condition):
    return condition.astype(BF16)


def cotangent_rows(grads, plan, counts, place):
    rows = grads.shape[0]
    lanes = lax.axis_size(WIDE)
    seg = rows // counts.shape[0]
    local = jnp.arange(rows, dtype=jnp.int32)
    slots = lax.dynamic_slice_in_dim(plan, place * rows, rows, 0)
    rank = jnp.sum((slots[None, :] < slots[:, None]).astype(jnp.int32), axis=1)
    owner = jnp.arange(plan.shape[0], dtype=jnp.int32) // rows
    held = plan[None, :] == (place * rows + local)[:, None]
    source = jnp.sum(jnp.where(held, owner[None, :], 0), axis=1)
    before = (source[None, :] == source[:, None]) & (local[None, :] < local[:, None])
    spot = source * (rows // lanes) + jnp.sum(before.astype(jnp.int32), axis=1)
    sent = jnp.dot(
        chosen(spot[None, :] == local[:, None]), grads, preferred_element_type=F32
    ).astype(BF16)
    back = exchange(sent, WIDE)
    live = local % seg < jnp.repeat(counts, seg, total_repeat_length=rows)
    pick = (rank[:, None] == local[None, :]) & live[:, None]
    return jnp.dot(chosen(pick), back, preferred_element_type=F32).astype(BF16)


def unit_order(slab, xl, ys, n, hidden):
    spans = slab.shape[0]
    per_span = hidden // spans
    units = n // (2 * spans)
    at = jnp.arange(ys * 2 * n, dtype=jnp.int32)
    y, core = at // (2 * n), at // n % 2
    gate, span, unit = at // (n // 2) % 2 == 0, at // units % spans, at % units
    k = ((y * 2 + xl) * 2 + core) * units + unit
    h = jnp.arange(hidden, dtype=jnp.int32)
    stored = jnp.repeat(slab, per_span, total_repeat_length=hidden)
    return chosen(
        gate[None, :]
        & (stored[:, None] == span[None, :])
        & ((h % per_span)[:, None] == k[None, :])
    )


def shards(x, grads, frozen, slab, down, up, counts, plan):
    ys = lax.axis_size("y")
    copies = lax.axis_size(DP)
    xl, core = lax.axis_index("xl"), lax.axis_index("core")
    rows, width = x.shape
    block, rank = down.shape
    hidden = up.shape[1]
    half = rows // 2
    n = 2 * frozen.shape[0] * frozen.shape[2]
    core_id = core.astype(jnp.int32).reshape(1)
    xl_id = xl.astype(jnp.int32).reshape(1)

    swapped = exchange(split_weights(frozen, ys, block), "core")
    chunks = swapped.shape[1]
    near = shift(down.T, "xl", 1)
    both_down = jnp.concatenate(
        [
            jnp.where(xl == half_at, down.T, near)
            .reshape(4, rank // 4, block)
            .transpose(1, 0, 2)
            .reshape(rank // 4, 4 * block)
            for half_at in range(2)
        ],
        axis=0,
    )
    sent = jnp.concatenate(
        [swapped.transpose(1, 0, 2, 3).reshape(chunks * 2 * n, 4 * block), both_down], axis=0
    )
    gathered = lax.all_gather(sent[None], "y", axis=0, tiled=True)

    own_a, own_b, other_a, other_b = split_rows(x, core_id, ys, block)
    next_own = shift(own_a, RING, 1)
    prev_own = shift(own_b, RING, -1)
    pair_a = shift(other_a, "core", 1)
    pair_b = shift(other_b, "core", 1)
    pair_a, pair_b, grads = lax.optimization_barrier((pair_a, pair_b, grads))
    next_pair = shift(pair_a, RING, 1)
    prev_pair = shift(pair_b, RING, -1)
    cot = cotangent_rows(grads, plan[0], counts, lax.axis_index(WIDE))
    cot_pair = shift(cot, "core", 1)
    cot_a = jnp.concatenate([cot[:half], cot_pair[:half]], axis=0)
    cot_b = jnp.concatenate([cot[half:], cot_pair[half:]], axis=0)
    cot_a, cot_b, next_own, prev_own = lax.optimization_barrier(
        (cot_a, cot_b, next_own, prev_own)
    )
    cots = [cot_a, shift(cot_b, RING, -1), shift(cot_a, RING, 1), cot_b]

    gathered, cots, pick = lax.optimization_barrier(
        (gathered, cots, unit_order(slab, xl, ys, n, hidden))
    )
    xs = [own_a, pair_a, prev_own, prev_pair, next_own, next_pair, own_b, pair_b]
    mine = products(xs, gathered, n, rank, block)
    his = shift(mine, "core", 1)
    plus, minus = gate_stage(mine, his, cots, pick, up, n)
    from_prev = shift(plus, RING, 1)
    from_next = shift(minus, RING, -1)

    terms = down_terms(xs, xl_id, plus, minus, from_next, from_prev, ys, block)
    lanes = terms.shape[-1]
    terms = exchange(terms.reshape(-1, 8, lanes), ("z", "y"))
    total = terms.astype(F32).sum(0).astype(BF16)
    full = exchange(jnp.tile(total[None], (copies, 1, 1)), DP)
    full = full.astype(F32).reshape(rank // 8, -1, 8, lanes).sum(1).reshape(rank, lanes)
    return full[:, :block].T, full[:, block:]


def solution(mesh):
    dp, wide = mesh.devices.shape
    fine = Mesh(mesh.devices.reshape(dp // 2, 2, wide // 4, 2, 2), EVERY)
    placed = (
        P(EVERY, None),
        P(EVERY, None),
        P(None, None, WIDE, None),
        P(),
        P(WIDE, None),
        P(),
        P(EVERY),
        P(DP, None),
    )
    return jax.shard_map(
        shards, mesh=fine, in_specs=placed, out_specs=(P(WIDE, None), P()), check_vma=False
    )
```

```python
import functools

import jax
import jax.numpy as jnp
from jax import lax
from jax.experimental import pallas as pl
from jax.experimental.pallas import tpu as pltpu
from jax.sharding import Mesh
from jax.sharding import PartitionSpec as P

F32 = jnp.float32
BF16 = jnp.bfloat16
DP = ("z", "xh")
WIDE = ("y", "xl", "core")
RING = ("xh", "xl")
EVERY = ("z", "xh", "y", "xl", "core")
MIB = 1024 * 1024
NT = (((1,), (1,)), ((), ()))
TN = (((0,), (0,)), ((), ()))


def shift(array, axes, step):
    size = lax.axis_size(axes)
    return lax.ppermute(array, axes, [(i, (i + step) % size) for i in range(size)])


def exchange(array, axes):
    return lax.all_to_all(array, axes, split_axis=0, concat_axis=0, tiled=True)


def params(mib):
    return pltpu.CompilerParams(vmem_limit_bytes=mib * MIB)


def split_rows_kernel(core_ref, x_ref, own_a, own_b, other_a, other_b, *, block):
    core = core_ref[0]
    half = x_ref.shape[0] // 2
    for xl in range(2):
        mine = pl.multiple_of(xl * 2 * block + core * block, block)
        his = pl.multiple_of(xl * 2 * block + (1 - core) * block, block)
        own_a[xl, 0] = x_ref[:half, pl.ds(mine, block)]
        own_b[xl, 0] = x_ref[half:, pl.ds(mine, block)]
        other_a[xl, 0] = x_ref[:half, pl.ds(his, block)]
        other_b[xl, 0] = x_ref[half:, pl.ds(his, block)]


def split_rows(x, core, ys, block):
    rows, width = x.shape
    half = rows // 2
    shape = jax.ShapeDtypeStruct((2, ys // 4, half, 4 * block), BF16)
    spec = pl.BlockSpec((2, 1, half, block), lambda y, c: (0, y // 4, 0, y % 4))
    parts = pl.pallas_call(
        functools.partial(split_rows_kernel, block=block),
        grid_spec=pltpu.PrefetchScalarGridSpec(
            num_scalar_prefetch=1,
            grid=(ys,),
            in_specs=[pl.BlockSpec((rows, 4 * block), lambda y, c: (0, y))],
            out_specs=[spec] * 4,
        ),
        out_shape=[shape] * 4,
        compiler_params=params(24),
        cost_estimate=pl.CostEstimate(flops=0, bytes_accessed=rows * width * 4, transcendentals=0),
        name="split_rows",
    )(core, x)
    return [part.reshape(2 * (ys // 4), half, 4 * block) for part in parts]


def split_weights_kernel(core_ref, w_ref, mine_ref, other_ref, *, block):
    spans = w_ref.shape[0]
    first = core_ref[0] == 0
    rows = jnp.concatenate([w_ref[s, j].astype(F32) for j in range(2) for s in range(spans)], axis=0)
    for xl in range(2):
        for y in range(4):
            at = (y * 2 + xl) * 2 * block
            even, odd = rows[:, at : at + block], rows[:, at + block : at + 2 * block]
            lanes = slice(y * block, (y + 1) * block)
            mine_ref[xl, 0, :, lanes] = jnp.where(first, even, odd).astype(BF16)
            other_ref[xl, 0, :, lanes] = jnp.where(first, odd, even).astype(BF16)


def split_weights(w, core, ys, block):
    spans, _, units, width = w.shape
    n = 2 * spans * units
    spec = pl.BlockSpec((2, 1, n, 4 * block), lambda y, c: (0, y, 0, 0))
    shape = jax.ShapeDtypeStruct((2, ys // 4, n, 4 * block), BF16)
    parts = pl.pallas_call(
        functools.partial(split_weights_kernel, block=block),
        grid_spec=pltpu.PrefetchScalarGridSpec(
            num_scalar_prefetch=1,
            grid=(ys // 4,),
            in_specs=[pl.BlockSpec((spans, 2, units, 16 * block), lambda y, c: (0, 0, 0, y))],
            out_specs=[spec, spec],
        ),
        out_shape=[shape, shape],
        compiler_params=params(24),
        cost_estimate=pl.CostEstimate(flops=0, bytes_accessed=w.size * 4, transcendentals=0),
        name="split_weights",
    )(core, w)
    return [part.reshape(2 * (ys // 4), n, 4 * block) for part in parts]


def products_kernel(*refs, block, rank, n):
    x_refs, (g_ref, out_ref, w_ref, down_ref, sems) = refs[:8], refs[8:]
    chunks = x_refs[0].shape[0]
    ys = g_ref.shape[0]
    copies = [
        pltpu.make_async_copy(g_ref.at[:, 2 * chunks * n :, :], down_ref, sems.at[chunks])
    ] + [
        pltpu.make_async_copy(
            g_ref.at[:, 2 * k * n : 2 * (k + 1) * n, :], w_ref.at[k], sems.at[k]
        )
        for k in range(chunks)
    ]
    for copy in copies:
        copy.start()
    copies[0].wait()
    units = ys * 2 * n
    part = rank // 4
    total = None
    for k in range(chunks):
        x = jnp.concatenate([r[k] for r in x_refs], axis=0)
        xl, first = divmod(k, chunks // 2)
        down = jnp.concatenate(
            [
                jnp.concatenate(
                    [
                        down_ref[
                            first * 4 + y,
                            xl * part : (xl + 1) * part,
                            t * block : (t + 1) * block,
                        ]
                        for t in range(4)
                    ],
                    axis=0,
                )
                for y in range(4)
            ],
            axis=1,
        )
        copies[k + 1].wait()
        w = jnp.concatenate([w_ref[k].reshape(units, -1), down], axis=0)
        more = lax.dot_general(w, x, NT, preferred_element_type=F32)
        total = more if total is None else total + more
    out_ref[:, : units + rank] = total.T
    out_ref[:, units + rank :] = jnp.zeros_like(out_ref[:, units + rank :])


def products(xs, gathered, n, rank, block):
    chunks, part, lanes = xs[0].shape
    ys = gathered.shape[0]
    units = ys * 2 * n
    columns = units + pl.cdiv(rank, 128) * 128
    vm = pl.BlockSpec(memory_space=pltpu.VMEM)
    return pl.pallas_call(
        functools.partial(products_kernel, block=block, rank=rank, n=n),
        in_specs=[vm] * 8 + [pl.BlockSpec(memory_space=pltpu.HBM)],
        out_specs=vm,
        out_shape=jax.ShapeDtypeStruct((8 * part, columns), F32),
        scratch_shapes=[
            pltpu.VMEM((chunks, ys, 2 * n, lanes), BF16),
            pltpu.VMEM((ys, rank // 2, lanes), BF16),
            pltpu.SemaphoreType.DMA((chunks + 1,)),
        ],
        compiler_params=params(49),
        cost_estimate=pl.CostEstimate(
            flops=2 * 8 * part * chunks * lanes * (units + rank),
            bytes_accessed=(8 * part + units + rank) * chunks * lanes * 2,
            transcendentals=0,
        ),
        name="products",
    )(*xs, gathered)


def swap_pairs(ref, part):
    return jnp.concatenate(
        [ref[(i ^ 1) * part : ((i ^ 1) + 1) * part] for i in range(8)], axis=0
    )


def gate_kernel(mine_ref, his_ref, a_ref, next_b_ref, prev_a_ref, b_ref, pick_ref, up_ref,
                plus_ref, minus_ref, *, n, part, rank):
    units = pick_ref.shape[1]
    total = mine_ref[...] + swap_pairs(his_ref, part)
    low = total[:, units : units + rank].astype(BF16)
    pick = pick_ref[...]
    up = jnp.dot(up_ref[...], pick, preferred_element_type=F32).astype(BF16)
    cot = jnp.concatenate(
        [a_ref[...], next_b_ref[...], prev_a_ref[...], b_ref[...]], axis=0
    )
    cot = jnp.dot(cot, pick, preferred_element_type=F32)
    both = total[:, :units]
    gate = both + jnp.dot(low, up, preferred_element_type=F32)
    upper = pltpu.roll(both, units - n // 2, 1)
    s = jax.nn.sigmoid(gate)
    grad = (cot * upper * s * (1.0 + gate * (1.0 - s))).astype(BF16)
    low_grad = lax.dot_general(grad, up, NT, preferred_element_type=F32)
    ordered = lax.dot_general(grad, pick, NT, preferred_element_type=F32).astype(BF16)
    up_grad = lax.dot_general(low, ordered, TN, preferred_element_type=F32)
    group = 4 * part
    pieces = [up_grad[:, i * rank : (i + 1) * rank] for i in range(up_grad.shape[1] // rank)]
    plus_ref[:, :rank] = low_grad[:group]
    plus_ref[:, rank:] = jnp.concatenate(pieces, axis=0)
    minus_ref[...] = low_grad[group:]


def gate_stage(mine, his, cots, pick, up, n):
    rows = mine.shape[0]
    rank, hidden = up.shape
    vm = pl.BlockSpec(memory_space=pltpu.VMEM)
    return pl.pallas_call(
        functools.partial(gate_kernel, n=n, part=rows // 8, rank=rank),
        in_specs=[vm] * 8,
        out_specs=[vm, vm],
        out_shape=[
            jax.ShapeDtypeStruct((rows // 2, 2 * rank), F32),
            jax.ShapeDtypeStruct((rows // 2, rank), F32),
        ],
        compiler_params=params(24),
        cost_estimate=pl.CostEstimate(
            flops=2 * rows * hidden * (2 * hidden + 3 * rank),
            bytes_accessed=rows * hidden * 12,
            transcendentals=rows * hidden,
        ),
        name="gate_stage",
    )(mine, his, *cots, pick, up)


def down_kernel(xl_ref, *refs, block):
    x_refs, (plus_ref, minus_ref, from_next, from_prev, out_ref) = refs[:8], refs[8:]
    rank = minus_ref.shape[1]
    low = jnp.concatenate(
        [plus_ref[:, :rank] + from_next[...], minus_ref[...] + from_prev[:, :rank]], axis=0
    ).astype(BF16)
    up = plus_ref[:, rank:] + from_prev[:, rank:]
    up = jnp.concatenate(
        [up[i * rank : (i + 1) * rank] for i in range(up.shape[0] // rank)], axis=1
    )
    per = x_refs[0].shape[0] // 2
    for k in range(per):
        x = jnp.concatenate([r[xl_ref[0] * per + k] for r in x_refs], axis=0)
        terms = lax.dot_general(low, x, TN, preferred_element_type=F32)
        for i in range(4):
            row = jnp.concatenate([terms[:, i * block : (i + 1) * block], up], axis=1)
            for g in range(rank // 8):
                out_ref[g, k * 4 + i] = row[g * 8 : (g + 1) * 8].astype(BF16)


def down_terms(xs, xl, plus, minus, from_next, from_prev, ys, block):
    group, rank = minus.shape
    hidden = group // rank * rank
    vm = pl.BlockSpec(memory_space=pltpu.VMEM)
    return pl.pallas_call(
        functools.partial(down_kernel, block=block),
        in_specs=[pl.BlockSpec(memory_space=pltpu.SMEM)] + [vm] * 12,
        out_specs=vm,
        out_shape=jax.ShapeDtypeStruct((rank // 8, ys, 8, block + hidden), BF16),
        compiler_params=params(24),
        cost_estimate=pl.CostEstimate(
            flops=2 * 2 * group * rank * ys * block,
            bytes_accessed=(2 * group + rank) * ys * block * 2,
            transcendentals=0,
        ),
        name="down_terms",
    )(xl, *xs, plus, minus, from_next, from_prev)


def chosen(condition):
    return condition.astype(BF16)


def cotangent_rows(grads, plan, counts, place):
    rows = grads.shape[0]
    lanes = lax.axis_size(WIDE)
    seg = rows // counts.shape[0]
    local = jnp.arange(rows, dtype=jnp.int32)
    slots = lax.dynamic_slice_in_dim(plan, place * rows, rows, 0)
    rank = jnp.sum((slots[None, :] < slots[:, None]).astype(jnp.int32), axis=1)
    owner = jnp.arange(plan.shape[0], dtype=jnp.int32) // rows
    held = plan[None, :] == (place * rows + local)[:, None]
    source = jnp.sum(jnp.where(held, owner[None, :], 0), axis=1)
    before = (source[None, :] == source[:, None]) & (local[None, :] < local[:, None])
    spot = source * (rows // lanes) + jnp.sum(before.astype(jnp.int32), axis=1)
    sent = jnp.dot(
        chosen(spot[None, :] == local[:, None]), grads, preferred_element_type=F32
    ).astype(BF16)
    back = exchange(sent, WIDE)
    live = local % seg < jnp.repeat(counts, seg, total_repeat_length=rows)
    pick = (rank[:, None] == local[None, :]) & live[:, None]
    return jnp.dot(chosen(pick), back, preferred_element_type=F32).astype(BF16)


def unit_order(slab, xl, ys, n, hidden):
    spans = slab.shape[0]
    per_span = hidden // spans
    units = n // (2 * spans)
    at = jnp.arange(ys * 2 * n, dtype=jnp.int32)
    y, core = at // (2 * n), at // n % 2
    gate, span, unit = at // (n // 2) % 2 == 0, at // units % spans, at % units
    k = ((y * 2 + xl) * 2 + core) * units + unit
    h = jnp.arange(hidden, dtype=jnp.int32)
    stored = jnp.repeat(slab, per_span, total_repeat_length=hidden)
    return chosen(
        gate[None, :]
        & (stored[:, None] == span[None, :])
        & ((h % per_span)[:, None] == k[None, :])
    )


def shards(x, grads, frozen, slab, down, up, counts, plan):
    ys = lax.axis_size("y")
    copies = lax.axis_size(DP)
    xl, core = lax.axis_index("xl"), lax.axis_index("core")
    rows, width = x.shape
    block, rank = down.shape
    hidden = up.shape[1]
    half = rows // 2
    n = 2 * frozen.shape[0] * frozen.shape[2]
    core_id = core.astype(jnp.int32).reshape(1)
    xl_id = xl.astype(jnp.int32).reshape(1)

    mine, other = split_weights(frozen, core_id, ys, block)
    other = shift(other, "core", 1)
    swapped = jnp.where(core == 0, jnp.stack([mine, other]), jnp.stack([other, mine]))
    chunks = swapped.shape[1]
    near = shift(down.T, "xl", 1)
    both_down = jnp.concatenate(
        [
            jnp.where(xl == half_at, down.T, near)
            .reshape(4, rank // 4, block)
            .transpose(1, 0, 2)
            .reshape(rank // 4, 4 * block)
            for half_at in range(2)
        ],
        axis=0,
    )
    sent = jnp.concatenate(
        [swapped.transpose(1, 0, 2, 3).reshape(chunks * 2 * n, 4 * block), both_down], axis=0
    )
    gathered = lax.all_gather(sent[None], "y", axis=0, tiled=True)

    own_a, own_b, other_a, other_b = split_rows(x, core_id, ys, block)
    next_own = shift(own_a, RING, 1)
    prev_own = shift(own_b, RING, -1)
    pair_a = shift(other_a, "core", 1)
    pair_b = shift(other_b, "core", 1)
    pair_a, pair_b, grads = lax.optimization_barrier((pair_a, pair_b, grads))
    next_pair = shift(pair_a, RING, 1)
    prev_pair = shift(pair_b, RING, -1)
    cot = cotangent_rows(grads, plan[0], counts, lax.axis_index(WIDE))
    cot_pair = shift(cot, "core", 1)
    cot_a = jnp.concatenate([cot[:half], cot_pair[:half]], axis=0)
    cot_b = jnp.concatenate([cot[half:], cot_pair[half:]], axis=0)
    cot_a, cot_b, next_own, prev_own = lax.optimization_barrier(
        (cot_a, cot_b, next_own, prev_own)
    )
    cots = [cot_a, shift(cot_b, RING, -1), shift(cot_a, RING, 1), cot_b]

    gathered, cots, pick = lax.optimization_barrier(
        (gathered, cots, unit_order(slab, xl, ys, n, hidden))
    )
    xs = [own_a, pair_a, prev_own, prev_pair, next_own, next_pair, own_b, pair_b]
    mine = products(xs, gathered, n, rank, block)
    his = shift(mine, "core", 1)
    plus, minus = gate_stage(mine, his, cots, pick, up, n)
    from_prev = shift(plus, RING, 1)
    from_next = shift(minus, RING, -1)

    terms = down_terms(xs, xl_id, plus, minus, from_next, from_prev, ys, block)
    lanes = terms.shape[-1]
    terms = exchange(terms.reshape(-1, 8, lanes), ("z", "y"))
    total = terms.astype(F32).sum(0).astype(BF16)
    full = exchange(jnp.tile(total[None], (copies, 1, 1)), DP)
    full = full.astype(F32).reshape(rank // 8, -1, 8, lanes).sum(1).reshape(rank, lanes)
    return full[:, :block].T, full[:, block:]


def solution(mesh):
    dp, wide = mesh.devices.shape
    fine = Mesh(mesh.devices.reshape(dp // 2, 2, wide // 4, 2, 2), EVERY)
    placed = (
        P(EVERY, None),
        P(EVERY, None),
        P(None, None, WIDE, None),
        P(),
        P(WIDE, None),
        P(),
        P(EVERY),
        P(DP, None),
    )
    return jax.shard_map(
        shards, mesh=fine, in_specs=placed, out_specs=(P(WIDE, None), P()), check_vma=False
    )
```
